128 devices in a mesh: tm: 16 (over z, y), chan: 8 (over x, core).
Axes of the slice: x: 4, y: 4, z: 4, core: 2. Of those that a mesh axis runs over, the one named last changes fastest.
Arguments:
- visibilities: bfloat16 [64, 4096, 2, 1024], P('tm', None, None, 'chan'), may hold values from -6 to 6
- owner_order: int32 [4096], replicated, may hold values from 0 to 4095, each once
- group_ids: int32 [4096], replicated, may hold values from 0 to 511, never falling along the last dimension, each value on 1 to 32 neighbouring positions
- partner_flags: int32 [4096, 8], replicated, may hold values 0 or 1
Outputs:
- pair_power: float32 [4096, 16, 1024], P(('tm', 'chan'))
The draws below stay inside these ranges and needn't reach their ends.
Inputs may be any that keep to these rules, and one draw needn't show every extreme that they name: `owner_order`: each slot holds a different correlator baseline. `group_ids`: never falls along slots; each group holds 1 to 32 slots, one exactly 32. `partner_flags`: a 1 in column k lists slot s + k + 1 for slot s.
All inputs are finite; a program needn't handle non-finite values.
Results may differ from the reference program's by a relative error of at most 0.0055.
Values may be sent and summed in bfloat16 or wider, within the bound.
No kernel may reach another device: no remote copies, remote signals or barrier semaphores. Data moves between devices by JAX's collectives and lax.ppermute only.
A program may use at most 128 MiB of HBM per device.

```python
import math
import jax
import jax.numpy as jnp
import numpy as np
from jax import lax

F = 1024
B_DEV = 32
REACH = 8
MOST = 32
TIMES = 64
BASE = 4096
GROUPS = 512


def touch_ends(values, key, smallest, largest):
    spot = [jax.random.randint(jax.random.fold_in(key, axis), (), 0, length) for axis, length in enumerate(values.shape)]
    widest = values.shape.index(max(values.shape))
    neighbour = spot[:widest] + [(spot[widest] + 1) % values.shape[widest]] + spot[widest + 1:]
    return values.at[tuple(spot)].set(smallest).at[tuple(neighbour)].set(largest)


def block_levels(own_key, extent, cuts, low, high):
    level, own = 1.0, jax.random.fold_in(own_key, 6)
    for axis_at, blocks in cuts:
        draws = jnp.exp(jax.random.uniform(jax.random.fold_in(own, axis_at), (blocks,), jnp.float32, low / len(cuts), high / len(cuts)))
        level = level * jnp.repeat(draws, extent[axis_at] // blocks).reshape([-1 if axis == axis_at else 1 for axis in range(len(extent))])
    return level


def split_up(number_of, total, most, skew):
    loads = [(1 << 20) // math.isqrt(standing ** skew) + 1 for standing in range(2, number_of + 1)]
    surplus, counts = total - most - (number_of - 1), [1] * (number_of - 1)
    while surplus > 0:
        movable = [i for i in range(number_of - 1) if counts[i] < most]
        mass, left = sum([loads[i] for i in movable]), surplus
        for i in movable:
            more = min(most - counts[i], max(1, left * loads[i] // mass), surplus)
            counts[i] = counts[i] + more
            surplus = surplus - more
    return np.array([most] + counts)


def uneven(rng, count, total, most, slope):
    if count == 2:
        one = jax.random.randint(rng, (), max(1, total - most), min(most, total - 1) + 1)
        return jnp.stack([one, total - one])
    tallies = jnp.asarray(split_up(count, total, most, slope), jnp.int32)
    pairs = (count - 1) // 2
    donor, receiver = tallies[1:1 + 2 * pairs:2], tallies[2:2 + 2 * pairs:2]
    margin = jnp.minimum(donor - 1, most - receiver)
    moved = jax.random.randint(jax.random.fold_in(rng, 1), (pairs,), 0, 1 << 20) % (margin + 1)
    tallies = tallies.at[1:1 + 2 * pairs:2].set(donor - moved).at[2:2 + 2 * pairs:2].set(receiver + moved)
    return tallies[jax.random.permutation(jax.random.fold_in(rng, 2), count)]


def noise(stream_key, extent, deviation, most, pieces=(), held_as=jnp.bfloat16):
    values = jax.random.normal(stream_key, extent, jnp.float32) * deviation
    if len(pieces) > 0:
        values = block_levels(stream_key, extent, pieces, -0.22, 0.18) * values
    return jnp.clip(values, min=-most, max=most).astype(held_as)


def setup_inputs(seed: int = 0) -> dict:
    arg_keys = jax.random.split(jax.random.key(seed), 5)
    visibilities = noise(arg_keys[0], (TIMES, BASE, 2, F), 1.0, 6.0, ((0, 16), (3, 8)))
    owner_order = jax.random.permutation(arg_keys[1], BASE).astype(jnp.int32)
    group_ids = jnp.searchsorted(jnp.cumsum(uneven(arg_keys[2], GROUPS, BASE, MOST, 2)), jnp.arange(BASE), side="right").astype(jnp.int32)
    partner_flags = touch_ends((jax.random.randint(arg_keys[3], (BASE, REACH), 0, 4) < 3).astype(jnp.int32), jax.random.fold_in(arg_keys[3], 1), 0, 1)
    return {"visibilities": visibilities, "owner_order": owner_order, "group_ids": group_ids, "partner_flags": partner_flags}


def delay_table(n_chan):
    channel_index = jnp.arange(n_chan, dtype=jnp.int32)
    phase_index = channel_index[:, None] * channel_index[None, :] % n_chan
    phase_angle = 2.0 * math.pi / n_chan * phase_index.astype(jnp.float32)
    base_angle = 2.0 * math.pi / n_chan * channel_index.astype(jnp.float32)
    window_taper = 0.35875 - 0.48829 * jnp.cos(base_angle) + 0.14128 * jnp.cos(2.0 * base_angle) - 0.01168 * jnp.cos(3.0 * base_angle)
    weights_norm = window_taper / jnp.sqrt(jnp.sum(window_taper * window_taper))
    cosine = weights_norm[:, None] * jnp.cos(phase_angle)
    sine_part = weights_norm[:, None] * jnp.sin(phase_angle)
    upper_half = jnp.concatenate([cosine, -sine_part], 1)
    bottom = jnp.concatenate([sine_part, cosine], 1)
    return jnp.concatenate([upper_half, bottom], 0).astype(jnp.bfloat16)

def pair_sum(row_spectra, partner_rows):
    summed = lax.optimization_barrier(jnp.sum(row_spectra.astype(jnp.float32) * partner_rows.astype(jnp.float32), axis=0))
    half_width = summed.shape[1] // 2
    return (summed[:, :half_width] + summed[:, half_width:]) / row_spectra.shape[0]

def reference(visibilities, owner_order, group_ids, partner_flags):
    n_times, n_base, _, n_chan = visibilities.shape
    reach = partner_flags.shape[1]
    n_blocks = n_base // B_DEV
    delay_matrix = delay_table(n_chan)
    ordered = jnp.take(visibilities, owner_order, axis=0 + 1)
    blocks = jnp.moveaxis(ordered.reshape(n_times, n_blocks, B_DEV, 2 * n_chan), 1, 0)

    def transform(block):
        flat = block.reshape(n_times * B_DEV, 2 * n_chan)
        result = jnp.dot(flat, delay_matrix, preferred_element_type=jnp.float32).astype(jnp.bfloat16)
        return result.reshape(n_times, B_DEV, 2 * n_chan)
    spectra = lax.map(transform, blocks)
    spectra = jnp.moveaxis(spectra, 0, 1).reshape(n_times, n_base, 2 * n_chan)
    padded = jnp.pad(spectra, ((0, 0), (reach, reach), (0, 0)))
    padded_groups = jnp.pad(group_ids, (reach, reach), constant_values=-1)
    padded_flags = jnp.pad(partner_flags, ((reach, reach), (0, 0)))

    def one_block(block_index):
        start = block_index * B_DEV
        extended = lax.dynamic_slice_in_dim(padded, start, B_DEV + 2 * reach, 1)
        group_window = lax.dynamic_slice_in_dim(padded_groups, start, B_DEV + 2 * reach, 0)
        flag_window = lax.dynamic_slice_in_dim(padded_flags, start, B_DEV + 2 * reach, 0)
        centre = extended[:, reach:reach + B_DEV]
        own_group = group_window[reach:reach + B_DEV]
        columns = []
        for offset in range(1, reach + 1):
            valid = (group_window[reach + offset:reach + offset + B_DEV] == own_group) & (flag_window[reach:reach + B_DEV, offset - 1] == 1)
            power = pair_sum(centre, extended[:, reach + offset:reach + offset + B_DEV])
            columns.append(jnp.where(valid[:, None], power, jnp.float32(0.0)))
        for offset in range(1, reach + 1):
            valid = (group_window[reach - offset:reach - offset + B_DEV] == own_group) & (flag_window[reach - offset:reach - offset + B_DEV, offset - 1] == 1)
            power = pair_sum(centre, extended[:, reach - offset:reach - offset + B_DEV])
            columns.append(jnp.where(valid[:, None], power, jnp.float32(0.0)))
        return jnp.stack(columns, 1)
    result = lax.map(one_block, jnp.arange(n_blocks, dtype=jnp.int32))
    return result.reshape(n_base, 2 * reach, n_chan)
```

```python
import functools
import math

import jax
import jax.numpy as jnp
from jax import lax
from jax.experimental import pallas as pl
from jax.experimental.pallas import tpu as pltpu
from jax.sharding import PartitionSpec as P

AXES = ("tm", "chan")
MIB = 2**20
LANES = 128
PARTS = (3, 1)


def delay_table(n_chan):
    channel_index = jnp.arange(n_chan, dtype=jnp.int32)
    phase_index = channel_index[:, None] * channel_index[None, :] % n_chan
    phase_angle = 2.0 * math.pi / n_chan * phase_index.astype(jnp.float32)
    base_angle = 2.0 * math.pi / n_chan * channel_index.astype(jnp.float32)
    window_taper = (
        0.35875
        - 0.48829 * jnp.cos(base_angle)
        + 0.14128 * jnp.cos(2.0 * base_angle)
        - 0.01168 * jnp.cos(3.0 * base_angle)
    )
    weights_norm = window_taper / jnp.sqrt(jnp.sum(window_taper * window_taper))
    cosine = weights_norm[:, None] * jnp.cos(phase_angle)
    sine_part = weights_norm[:, None] * jnp.sin(phase_angle)
    upper_half = jnp.concatenate([cosine, -sine_part], 1)
    bottom = jnp.concatenate([sine_part, cosine], 1)
    return jnp.concatenate([upper_half, bottom], 0).astype(jnp.bfloat16)


def gather_kernel(order_ref, vis_ref, out_ref):
    owners, count, per = out_ref.shape[:3]
    first = pl.program_id(0) * owners

    def one_owner(owner, carry):
        base = (first + owner) * per
        for j in range(per):
            source = order_ref[base + j]
            for t in range(count):
                out_ref[owner, t, j] = vis_ref[t, source]
        return carry

    lax.fori_loop(0, owners, one_owner, 0)


def gather(visibilities, order, first, count, n_dev):
    n_base = visibilities.shape[1]
    per = n_base // n_dev
    tail = visibilities.shape[2:]
    steps = 8
    part = lax.slice_in_dim(visibilities, first, first + count, axis=0)
    return pl.pallas_call(
        gather_kernel,
        grid_spec=pltpu.PrefetchScalarGridSpec(
            num_scalar_prefetch=1,
            grid=(steps,),
            in_specs=[pl.BlockSpec((count, n_base) + tail, lambda i, o: (0, 0, 0, 0))],
            out_specs=pl.BlockSpec(
                (n_dev // steps, count, per) + tail, lambda i, o: (i, 0, 0, 0, 0)
            ),
        ),
        out_shape=jax.ShapeDtypeStruct((n_dev, count, per) + tail, visibilities.dtype),
        compiler_params=pltpu.CompilerParams(vmem_limit_bytes=40 * MIB),
        cost_estimate=pl.CostEstimate(
            flops=0, bytes_accessed=2 * count * n_base * 512, transcendentals=0
        ),
        name="slot_gather",
    )(order, part)


def spectra_kernel(received_ref, order_ref, table_ref, out_ref, rows_ref):
    sources, n_chan, _, pairs = received_ref.shape[:4]
    half = table_ref.shape[0] // 2
    group = order_ref.shape[0] // 2
    for b in range(pairs // 16):
        block = jnp.concatenate(
            [
                received_ref[:, c, 0, pl.ds(16 * b, 16), :].reshape(2 * group, LANES)
                for c in range(n_chan)
            ],
            axis=1,
        )
        sorted_rows = jnp.dot(
            order_ref[...], block, preferred_element_type=jnp.float32
        ).astype(jnp.bfloat16)
        rows_ref[pl.ds(b * group, group), pl.ds(0, half)] = sorted_rows[:group]
        rows_ref[pl.ds(b * group, group), pl.ds(half, half)] = sorted_rows[group:]
    width = 512
    for n in range(2 * half // width):
        part = jnp.dot(
            rows_ref[...],
            table_ref[:, pl.ds(n * width, width)],
            preferred_element_type=jnp.float32,
        ).astype(jnp.bfloat16)
        out_ref[0, :, :, pl.ds(n * width, width)] = part.reshape(
            pairs // 2, sources, width
        )


def spectra(received, row_order, table, n_tm, n_chan):
    _, count, pairs, lanes = received.shape
    rows = n_tm * pairs // 2
    width = table.shape[1]
    return pl.pallas_call(
        spectra_kernel,
        grid=(count,),
        in_specs=[
            pl.BlockSpec((n_tm, n_chan, 1, pairs, lanes), lambda t: (0, 0, t, 0, 0)),
            pl.BlockSpec(row_order.shape, lambda t: (0, 0)),
            pl.BlockSpec(table.shape, lambda t: (0, 0), pipeline_mode=pl.Buffered(1)),
        ],
        out_specs=pl.BlockSpec((1, pairs // 2, n_tm, width), lambda t: (t, 0, 0, 0)),
        out_shape=jax.ShapeDtypeStruct((count, pairs // 2, n_tm, width), jnp.bfloat16),
        scratch_shapes=[pltpu.VMEM((rows, width), jnp.bfloat16)],
        compiler_params=pltpu.CompilerParams(vmem_limit_bytes=40 * MIB),
        cost_estimate=pl.CostEstimate(
            flops=2 * count * rows * width * width,
            bytes_accessed=4 * count * rows * width + 2 * width * width,
            transcendentals=0,
        ),
        name="delay_spectra",
    )(received.reshape(n_tm, n_chan, count, pairs, lanes), row_order, table)


def pair_kernel(last, refs_in, refs_out, scratch):
    real_ref, imag_ref = scratch[:2]
    reach, per = 8, 32
    count = refs_in[0].shape[0]
    times = refs_in[0].shape[2]
    for which, target in ((0, real_ref), (1, imag_ref)):
        before, own, after = refs_in[3 * which : 3 * which + 3]
        for t in range(count):
            span = pl.ds(t * times, times)
            target[pl.ds(0, reach), span] = before[t].astype(jnp.float32)
            target[pl.ds(reach, per), span] = own[t].astype(jnp.float32)
            target[pl.ds(reach + per, reach), span] = after[t].astype(jnp.float32)
    column = lax.broadcasted_iota(jnp.int32, (reach, LANES), 0)
    power_ref = scratch[2] if last else refs_out[0]

    def one_slot(s, carry):
        real, imag = real_ref[s], imag_ref[s]
        powers = jnp.zeros((reach, LANES), jnp.float32)
        for k in range(1, reach + 1):
            product = real * real_ref[s + k] + imag * imag_ref[s + k]
            powers = jnp.where(
                column == k - 1, jnp.sum(product, axis=0, keepdims=True), powers
            )
        if last:
            powers = (powers + refs_in[6][s]) * (1.0 / 64.0)
            powers = jnp.where(refs_in[7][s] > 0.0, powers, 0.0)
        power_ref[s] = powers
        return carry

    lax.fori_loop(0, reach + per, one_slot, 0)
    if last:
        out_ref = refs_out[0]

        def one_output(s, carry):
            out_ref[s, pl.ds(0, reach), :] = power_ref[s + reach]
            backward = power_ref[s + reach - 1]
            for k in range(2, reach + 1):
                backward = jnp.where(column == k - 1, power_ref[s + reach - k], backward)
            out_ref[s, pl.ds(reach, reach), :] = backward
            return carry

        lax.fori_loop(0, per, one_output, 0)


def pair_powers(own, before, after, total=None, valid=None):
    count, per, times, width = own.shape
    reach = before.shape[1]
    chunks = width // 2 // LANES
    last = total is not None
    specs, operands = [], []
    for which in range(2):
        for array in (before, own, after):
            specs.append(
                pl.BlockSpec(
                    array.shape[:3] + (LANES,),
                    functools.partial(lambda w, j: (0, 0, 0, w * chunks + j), which),
                )
            )
            operands.append(array)
    power_spec = pl.BlockSpec((reach + per, reach, LANES), lambda j: (0, 0, j))
    power_shape = (reach + per, reach, width // 2)
    scratch = [pltpu.VMEM((per + 2 * reach, count * times, LANES), jnp.float32)] * 2
    if last:
        specs += [power_spec, pl.BlockSpec(valid.shape, lambda j: (0, 0, 0))]
        operands += [total, valid]
        scratch.append(pltpu.VMEM((reach + per, reach, LANES), jnp.float32))
        out_spec = pl.BlockSpec((per, 2 * reach, LANES), lambda j: (0, 0, j))
        out_shape = (per, 2 * reach, width // 2)
    else:
        out_spec, out_shape = power_spec, power_shape
    n_in = len(operands)

    def kernel(*refs):
        pair_kernel(last, refs[:n_in], refs[n_in : n_in + 1], refs[n_in + 1 :])

    return pl.pallas_call(
        kernel,
        grid=(chunks,),
        in_specs=specs,
        out_specs=out_spec,
        out_shape=jax.ShapeDtypeStruct(out_shape, jnp.float32),
        scratch_shapes=scratch,
        compiler_params=pltpu.CompilerParams(vmem_limit_bytes=40 * MIB),
        cost_estimate=pl.CostEstimate(
            flops=2 * (per + reach) * reach * count * times * width,
            bytes_accessed=2 * count * times * (per + 2 * reach) * width,
            transcendentals=0,
        ),
        name="pair_powers",
    )(*operands)


def body(visibilities, owner_order, group_ids, partner_flags):
    n_tm = lax.axis_size("tm")
    n_chan = lax.axis_size("chan")
    n_dev = n_tm * n_chan
    n_base = visibilities.shape[1]
    reach = partner_flags.shape[1]
    per = n_base // n_dev
    chan_total = visibilities.shape[3] * n_chan

    place = jnp.arange(n_tm * 16, dtype=jnp.int32)
    wanted = (place % n_tm) * 16 + (place // n_tm % 8) * 2 + place // (n_tm * 8)
    row_order = (wanted[:, None] == place[None, :]).astype(jnp.bfloat16)
    table = delay_table(chan_total)

    start = lax.axis_index(AXES) * per
    groups = lax.dynamic_slice_in_dim(
        jnp.pad(group_ids, (reach, reach), constant_values=-1), start, per + 2 * reach, 0
    )
    flags = lax.dynamic_slice_in_dim(
        jnp.pad(partner_flags, ((reach, reach), (0, 0))), start, per + reach, 0
    )
    own_group = groups[: per + reach]
    same = jnp.stack([groups[k : k + per + reach] == own_group for k in range(1, reach + 1)], 1)
    valid = jnp.broadcast_to(
        (same & (flags == 1)).astype(jnp.float32)[:, :, None], (per + reach, reach, LANES)
    )

    total = None
    first = 0
    up = [(i, i + 1) for i in range(n_dev - 1)]
    down = [(i + 1, i) for i in range(n_dev - 1)]
    for number, count in enumerate(PARTS):
        send = gather(visibilities, owner_order, first, count, n_dev)
        send = send.reshape(n_dev, count, 2 * per, visibilities.shape[3])
        received = lax.all_to_all(send, AXES, 0, 0, tiled=True)
        own = spectra(received, row_order, table, n_tm, n_chan)
        before = lax.ppermute(own[:, per - reach :], AXES, up)
        after = lax.ppermute(own[:, :reach], AXES, down)
        if number + 1 < len(PARTS):
            total = pair_powers(own, before, after)
        else:
            total = pair_powers(own, before, after, total, valid)
        first += count
    return total


def solution(mesh):
    return jax.shard_map(
        body,
        mesh=mesh,
        in_specs=(P("tm", None, None, "chan"), P(), P(), P()),
        out_specs=P(AXES, None, None),
        check_vma=False,
    )
```

```python
import functools
import math

import jax
import jax.numpy as jnp
from jax import lax
from jax.experimental import pallas as pl
from jax.experimental.pallas import tpu as pltpu
from jax.sharding import PartitionSpec as P

AXES = ("tm", "chan")
MIB = 2**20
LANES = 128
REACH = 8
OUTER = tuple(range(8)) + tuple(range(24, 32))
INNER = tuple(range(8, 24))


def in_hbm(array):
    return pltpu.with_memory_space_constraint(array, pltpu.HBM)


def half_table(n_chan):
    channel_index = jnp.arange(n_chan, dtype=jnp.int32)
    place = jnp.arange(n_chan, dtype=jnp.int32)
    delay_index = place // (2 * LANES) * LANES + place % LANES
    is_sine = place % (2 * LANES) >= LANES
    middle = is_sine & (delay_index == 0)
    delay_index = jnp.where(middle, n_chan // 2, delay_index)
    turn = jnp.where(is_sine & ~middle, 3 * n_chan // 4, 0)
    phase_index = (channel_index[:, None] * delay_index[None, :] + turn[None, :]) % n_chan
    phase_angle = 2.0 * math.pi / n_chan * phase_index.astype(jnp.float32)
    base_angle = 2.0 * math.pi / n_chan * channel_index.astype(jnp.float32)
    window_taper = (
        0.35875
        - 0.48829 * jnp.cos(base_angle)
        + 0.14128 * jnp.cos(2.0 * base_angle)
        - 0.01168 * jnp.cos(3.0 * base_angle)
    )
    weights_norm = window_taper / jnp.sqrt(jnp.sum(window_taper * window_taper))
    return (weights_norm[:, None] * jnp.cos(phase_angle)).astype(jnp.bfloat16)


def gather_kernel(slots, per, order_ref, vis_ref, _, out_ref):
    owners, count = out_ref.shape[0], out_ref.shape[2]
    first = pl.program_id(0) * owners

    def one_owner(owner, carry):
        base = (first + owner) * per
        for j, slot in enumerate(slots):
            source = order_ref[base + slot]
            for t in range(count):
                out_ref[owner, j, t] = vis_ref[t, source]
        return carry

    lax.fori_loop(0, owners, one_owner, 0)


def gather(visibilities, order, slots, n_dev, earlier):
    count, n_base = visibilities.shape[:2]
    tail = visibilities.shape[2:]
    steps = 8
    return pl.pallas_call(
        functools.partial(gather_kernel, slots, n_base // n_dev),
        grid_spec=pltpu.PrefetchScalarGridSpec(
            num_scalar_prefetch=1,
            grid=(steps,),
            in_specs=[
                pl.BlockSpec(memory_space=pltpu.VMEM),
                pl.BlockSpec(memory_space=pl.ANY),
            ],
            out_specs=pl.BlockSpec(
                (n_dev // steps, len(slots), count) + tail, lambda i, o: (i, 0, 0, 0, 0)
            ),
        ),
        out_shape=pltpu.HBM((n_dev, len(slots), count) + tail, visibilities.dtype),
        compiler_params=pltpu.CompilerParams(vmem_limit_bytes=24 * MIB),
        cost_estimate=pl.CostEstimate(
            flops=0, bytes_accessed=2 * count * n_dev * len(slots) * 512, transcendentals=0
        ),
        name="slot_gather",
    )(in_hbm(order), visibilities, in_hbm(earlier))


def spectra_kernel(received_ref, table_ref, out_ref):
    sources, n_chan, rows = received_ref.shape[:3]
    slots = out_ref.shape[2]
    n_rows = sources * rows
    block = jnp.concatenate(
        [received_ref[:, c].reshape(n_rows, LANES) for c in range(n_chan)], axis=1
    )
    chunks = table_ref.shape[1] // (2 * LANES)
    shape = (n_rows // 8, 8, LANES)
    first = lax.broadcasted_iota(jnp.int32, shape, 2) == 0
    is_real = lax.broadcasted_iota(jnp.int32, shape, 1) % 2 == 0

    def store(sign, c, value):
        value = jnp.swapaxes(value.reshape(sources, slots, 8, LANES), 0, 1)
        value = value.reshape(slots, sources * 8, LANES).astype(jnp.bfloat16)
        out_ref[sign, c] = value

    minus = []
    for c in range(chunks):
        both = jnp.dot(
            block, table_ref[:, pl.ds(2 * c * LANES, 2 * LANES)], preferred_element_type=jnp.float32
        )
        cosine, sine = both[:, :LANES].reshape(shape), both[:, LANES:].reshape(shape)
        other = jnp.where(is_real, pltpu.roll(sine, 7, 1), -pltpu.roll(sine, 1, 1))
        ahead, back = cosine + other, cosine - other
        if c == 0:
            ahead, back = jnp.where(first, cosine, ahead), jnp.where(first, sine, back)
        store(0, c, ahead)
        minus.append(back)
        if c > 0:
            store(1, c - 1, jnp.where(first, back, minus[c - 1]))
    store(1, chunks - 1, jnp.where(first, minus[0], minus[-1]))


def spectra(received, table, n_tm, n_chan):
    _, pairs, lanes = received.shape
    slots = pairs // 8
    step = REACH
    width = table.shape[1]
    rows = n_tm * 8
    chunks = width // (2 * LANES)
    return pl.pallas_call(
        spectra_kernel,
        grid=(slots // step,),
        in_specs=[
            pl.BlockSpec((n_tm, n_chan, 8 * step, lanes), lambda t: (0, 0, t, 0)),
            pl.BlockSpec(table.shape, lambda t: (0, 0), pipeline_mode=pl.Buffered(1)),
        ],
        out_specs=pl.BlockSpec((2, chunks, step, rows, LANES), lambda t: (0, 0, t, 0, 0)),
        out_shape=pltpu.HBM((2, chunks, slots, rows, LANES), jnp.bfloat16),
        compiler_params=pltpu.CompilerParams(vmem_limit_bytes=32 * MIB),
        cost_estimate=pl.CostEstimate(
            flops=2 * pairs * n_tm * width * width,
            bytes_accessed=8 * pairs * n_tm * width,
            transcendentals=0,
        ),
        name="delay_spectra",
    )(in_hbm(received.reshape(n_tm, n_chan, pairs, lanes)), in_hbm(table))


def fold_rows(sums):
    row = lax.broadcasted_iota(jnp.int32, sums[0].shape, 0)
    for bit in (1, 2, 4):
        low = (row & bit) == 0
        merged = []
        for i in range(0, len(sums), 2):
            a, b = sums[i], sums[i + 1]
            kept, moved = jnp.where(low, a, b), jnp.where(low, b, a)
            merged.append(kept + pltpu.roll(moved, 8 - bit, 0))
        sums = merged
    return sums[0]


def cross_tile(rows_ref, s, offsets):
    spans = [pl.ds(8 * g, 8) for g in range(rows_ref.shape[1] // 8)]
    own = [rows_ref[s, span] for span in spans]
    sums = []
    for k in range(1, REACH + 1):
        if k not in offsets:
            sums.append(jnp.zeros((8, LANES), jnp.float32))
            continue
        total = None
        for g, span in enumerate(spans):
            term = own[g] * rows_ref[s + k, span]
            total = term if total is None else total + term
        sums.append(total)
    return fold_rows(sums)


def load_rows(target, at, source):
    target[pl.ds(at, source.shape[0])] = source[...].astype(jnp.float32)


def outer_kernel(rows_in, out_ref, rows_ref):
    load_rows(rows_ref, 0, rows_in.at[0, 0])
    run = out_ref.shape[1] // 2

    def one_run(i, carry):
        for j in range(run):
            s = i * run + j
            out_ref[0, s] = cross_tile(rows_ref, s, range(1, run - j))
        return carry

    lax.fori_loop(0, 2, one_run, 0)


def edge_kernel(own, after, before, _, plus_ref, minus_ref, rows_ref):
    sign = pl.program_id(0)

    @pl.when(sign == 0)
    def _():
        load_rows(rows_ref, 0, own.at[0, 0])
        load_rows(rows_ref, REACH, after.at[0])

    @pl.when(sign == 1)
    def _():
        load_rows(rows_ref, 0, before.at[0])
        load_rows(rows_ref, REACH, own.at[0, 0])

    tiles = [cross_tile(rows_ref, j, range(REACH - j, REACH + 1)) for j in range(REACH)]

    @pl.when(sign == 0)
    def _():
        for j in range(REACH):
            plus_ref[0, j] = tiles[j]

    @pl.when(sign == 1)
    def _():
        for j in range(REACH):
            minus_ref[0, j] = tiles[j]


def final_kernel(
    outer, inner, sums_ref, plus_ref, minus_ref, left_ref, right_ref, valid_ref,
    out_ref, rows_ref,
):
    shape = (REACH, LANES)
    lane = lax.broadcasted_iota(jnp.int32, shape, 1)
    row = lax.broadcasted_iota(jnp.int32, shape, 0)
    mirror = pl.program_id(0) == 1
    order = jnp.where(mirror, (LANES - lane) % LANES, lane)
    slots = out_ref.shape[0]
    load_rows(rows_ref, 0, outer.at[0, 0, pl.ds(0, REACH)])
    load_rows(rows_ref, REACH, inner.at[0, 0])
    load_rows(rows_ref, slots - REACH, outer.at[0, 0, pl.ds(REACH, REACH)])
    powers = {}
    for s in range(-REACH, slots):
        terms = []
        if s < 0:
            terms.append(jnp.where(mirror, minus_ref[0, s + REACH], left_ref[0, s + REACH]))
        if s in OUTER:
            terms.append(sums_ref[0, OUTER.index(s)])
        if 0 <= s < slots - REACH:
            terms.append(cross_tile(rows_ref, s, range(max(1, REACH - s), REACH + 1)))
        if s >= slots - REACH:
            j = s - (slots - REACH)
            terms.append(jnp.where(mirror, right_ref[0, j], plus_ref[0, j]))
        value = jnp.take_along_axis(sum(terms[1:], terms[0]), order, axis=1)
        powers[s] = jnp.where(valid_ref[s + REACH] > 0.0, value * (1.0 / 64.0), 0.0)
        if s >= 0:
            out_ref[s, pl.ds(0, REACH), :] = powers[s]
            backward = powers[s - 1]
            for k in range(2, REACH + 1):
                backward = jnp.where(row == k - 1, powers[s - k], backward)
            out_ref[s, pl.ds(REACH, REACH), :] = backward


CHUNKS = 4


def cross_call(kernel, name, operands, specs, out_specs, out_shape, held, pairs):
    rows = 128
    return pl.pallas_call(
        kernel,
        grid=(2, CHUNKS),
        in_specs=specs,
        out_specs=out_specs,
        out_shape=out_shape,
        scratch_shapes=[pltpu.VMEM((held, rows, LANES), jnp.float32)],
        compiler_params=pltpu.CompilerParams(vmem_limit_bytes=24 * MIB),
        cost_estimate=pl.CostEstimate(
            flops=2 * pairs * rows * 1024,
            bytes_accessed=2 * held * rows * 1024,
            transcendentals=0,
        ),
        name=name,
    )(*operands)


def spectra_spec(slots, rows, place=lambda i: 0):
    return pl.BlockSpec((1, 1, slots, rows, LANES), lambda i, j: (i, j, place(i), 0, 0))


def sums_spec(slots):
    return pl.BlockSpec((1, slots, REACH, LANES), lambda i, j: (i * CHUNKS + j, 0, 0, 0))


def plus_spec(rows=REACH):
    return pl.BlockSpec(
        (1, REACH, rows, LANES), lambda i, j: (jnp.where(i == 0, j, CHUNKS - 1), 0, 0, 0)
    )


def minus_spec(rows=REACH):
    return pl.BlockSpec((1, REACH, rows, LANES), lambda i, j: (jnp.where(i == 0, 0, j), 0, 0, 0))


def outer_powers(outer):
    slots, rows = outer.shape[2:4]
    shape = jax.ShapeDtypeStruct((2 * CHUNKS, slots, REACH, LANES), jnp.float32)
    return cross_call(
        outer_kernel,
        "outer_pairs",
        [in_hbm(outer)],
        [spectra_spec(slots, rows)],
        sums_spec(slots),
        shape,
        slots,
        56,
    )


def edge_powers(outer, after, before, outer_sums):
    slots, rows = outer.shape[2:4]
    last = slots // REACH - 1
    shape = jax.ShapeDtypeStruct((CHUNKS, REACH, REACH, LANES), jnp.float32)
    return cross_call(
        edge_kernel,
        "edge_pairs",
        [in_hbm(outer), after, before, outer_sums],
        [
            spectra_spec(REACH, rows, lambda i: (1 - i) * last),
            plus_spec(rows),
            minus_spec(rows),
            pl.BlockSpec(memory_space=pl.ANY),
        ],
        [plus_spec(), minus_spec()],
        [shape, shape],
        2 * REACH,
        36,
    )


def final_powers(outer, inner, outer_sums, plus, minus, left, right, valid):
    rows = outer.shape[3]
    slots = 4 * REACH
    return cross_call(
        final_kernel,
        "pair_power",
        [in_hbm(outer), in_hbm(inner), outer_sums, plus, minus, left, right, valid],
        [
            spectra_spec(outer.shape[2], rows),
            spectra_spec(inner.shape[2], rows),
            sums_spec(outer_sums.shape[1]),
            plus_spec(),
            minus_spec(),
            plus_spec(),
            minus_spec(),
            pl.BlockSpec(valid.shape, lambda i, j: (0, 0, 0)),
        ],
        pl.BlockSpec(
            (slots, 2 * REACH, LANES),
            lambda i, j: (0, 0, jnp.where(i == 0, j, 2 * CHUNKS - 1 - j)),
        ),
        jax.ShapeDtypeStruct((slots, 2 * REACH, 2 * CHUNKS * LANES), jnp.float32),
        slots,
        164,
    )


def body(visibilities, owner_order, group_ids, partner_flags):
    n_tm = lax.axis_size("tm")
    n_chan = lax.axis_size("chan")
    n_dev = n_tm * n_chan
    count, n_base, _, width = visibilities.shape
    per = n_base // n_dev

    table = half_table(width * n_chan)

    start = lax.axis_index(AXES) * per
    groups = lax.dynamic_slice_in_dim(
        jnp.pad(group_ids, (REACH, REACH), constant_values=-1), start, per + 2 * REACH, 0
    )
    flags = lax.dynamic_slice_in_dim(
        jnp.pad(partner_flags, ((REACH, REACH), (0, 0))), start, per + REACH, 0
    )
    own_group = groups[: per + REACH]
    same = jnp.stack([groups[k : k + per + REACH] == own_group for k in range(1, REACH + 1)], 1)
    valid = jnp.broadcast_to(
        (same & (flags == 1)).astype(jnp.float32)[:, :, None], (per + REACH, REACH, LANES)
    )

    def exchange(slots, earlier):
        send = gather(visibilities, owner_order, slots, n_dev, earlier)
        send = send.reshape(n_dev, 2 * count * len(slots), width)
        return lax.all_to_all(send, AXES, 0, 0, tiled=True)

    up = [(i, i + 1) for i in range(n_dev - 1)]
    down = [(i + 1, i) for i in range(n_dev - 1)]
    received_outer = exchange(OUTER, group_ids)
    received_inner = exchange(INNER, table)
    outer = spectra(received_outer, table, n_tm, n_chan)
    after = lax.ppermute(outer[0, :, :REACH], AXES, down)
    before = lax.ppermute(outer[1, :, REACH:], AXES, up)
    outer_sums = outer_powers(outer)
    plus, minus = edge_powers(outer, after, before, outer_sums)
    left = lax.ppermute(plus, AXES, up)
    right = lax.ppermute(minus, AXES, down)
    inner = spectra(received_inner, table, n_tm, n_chan)
    return final_powers(outer, inner, outer_sums, plus, minus, left, right, valid)


def solution(mesh):
    return jax.shard_map(
        body,
        mesh=mesh,
        in_specs=(P("tm", None, None, "chan"), P(), P(), P()),
        out_specs=P(AXES, None, None),
        check_vma=False,
    )
```

```python
import functools
import math

import jax
import jax.numpy as jnp
from jax import lax
from jax.experimental import pallas as pl
from jax.experimental.pallas import tpu as pltpu
from jax.sharding import PartitionSpec as P

AXES = ("tm", "chan")
MIB = 2**20
LANES = 128
REACH = 8
OUTER = tuple(range(8)) + tuple(range(24, 32))
INNER = tuple(range(8, 24))


def in_hbm(array):
    return pltpu.with_memory_space_constraint(array, pltpu.HBM)


def half_table(n_chan):
    channel_index = jnp.arange(n_chan, dtype=jnp.int32)
    place = jnp.arange(n_chan, dtype=jnp.int32)
    delay_index = place // (2 * LANES) * LANES + place % LANES
    is_sine = place % (2 * LANES) >= LANES
    middle = is_sine & (delay_index == 0)
    delay_index = jnp.where(middle, n_chan // 2, delay_index)
    turn = jnp.where(is_sine & ~middle, 3 * n_chan // 4, 0)
    phase_index = (channel_index[:, None] * delay_index[None, :] + turn[None, :]) % n_chan
    phase_angle = 2.0 * math.pi / n_chan * phase_index.astype(jnp.float32)
    base_angle = 2.0 * math.pi / n_chan * channel_index.astype(jnp.float32)
    window_taper = (
        0.35875
        - 0.48829 * jnp.cos(base_angle)
        + 0.14128 * jnp.cos(2.0 * base_angle)
        - 0.01168 * jnp.cos(3.0 * base_angle)
    )
    weights_norm = window_taper / jnp.sqrt(jnp.sum(window_taper * window_taper))
    return (weights_norm[:, None] * jnp.cos(phase_angle)).astype(jnp.bfloat16)


def gather_kernel(slots, per, order_ref, vis_ref, _, out_ref):
    owners, count = out_ref.shape[0], out_ref.shape[2]
    first = pl.program_id(0) * owners

    def one_owner(owner, carry):
        base = (first + owner) * per
        for j, slot in enumerate(slots):
            source = order_ref[base + slot]
            for t in range(count):
                out_ref[owner, j, t] = vis_ref[t, source]
        return carry

    lax.fori_loop(0, owners, one_owner, 0)


def gather(visibilities, order, slots, n_dev, earlier):
    count, n_base = visibilities.shape[:2]
    tail = visibilities.shape[2:]
    steps = 8
    return pl.pallas_call(
        functools.partial(gather_kernel, slots, n_base // n_dev),
        grid_spec=pltpu.PrefetchScalarGridSpec(
            num_scalar_prefetch=1,
            grid=(steps,),
            in_specs=[
                pl.BlockSpec(memory_space=pltpu.VMEM),
                pl.BlockSpec(memory_space=pl.ANY),
            ],
            out_specs=pl.BlockSpec(
                (n_dev // steps, len(slots), count) + tail, lambda i, o: (i, 0, 0, 0, 0)
            ),
        ),
        out_shape=pltpu.HBM((n_dev, len(slots), count) + tail, visibilities.dtype),
        compiler_params=pltpu.CompilerParams(vmem_limit_bytes=24 * MIB),
        cost_estimate=pl.CostEstimate(
            flops=0, bytes_accessed=2 * count * n_dev * len(slots) * 512, transcendentals=0
        ),
        name="slot_gather",
    )(in_hbm(order), visibilities, in_hbm(earlier))


def spectra_kernel(received_ref, table_ref, _, out_ref):
    sources, n_chan, rows = received_ref.shape[:3]
    slots = out_ref.shape[2]
    n_rows = sources * rows
    block = jnp.concatenate(
        [received_ref[:, c].reshape(n_rows, LANES) for c in range(n_chan)], axis=1
    )
    chunks = table_ref.shape[1] // (2 * LANES)
    shape = (n_rows // 8, 8, LANES)
    first = lax.broadcasted_iota(jnp.int32, shape, 2) == 0
    is_real = lax.broadcasted_iota(jnp.int32, shape, 1) % 2 == 0

    def store(sign, c, value):
        value = jnp.swapaxes(value.reshape(sources, slots, 8, LANES), 0, 1)
        value = value.reshape(slots, sources * 8, LANES).astype(jnp.bfloat16)
        out_ref[sign, c] = value

    minus = []
    for c in range(chunks):
        both = jnp.dot(
            block, table_ref[:, pl.ds(2 * c * LANES, 2 * LANES)], preferred_element_type=jnp.float32
        )
        cosine, sine = both[:, :LANES].reshape(shape), both[:, LANES:].reshape(shape)
        other = jnp.where(is_real, pltpu.roll(sine, 7, 1), -pltpu.roll(sine, 1, 1))
        ahead, back = cosine + other, cosine - other
        if c == 0:
            ahead, back = jnp.where(first, cosine, ahead), jnp.where(first, sine, back)
        store(0, c, ahead)
        minus.append(back)
        if c > 0:
            store(1, c - 1, jnp.where(first, back, minus[c - 1]))
    store(1, chunks - 1, jnp.where(first, minus[0], minus[-1]))


def spectra(received, table, n_tm, n_chan, first, slots, earlier):
    _, pairs, lanes = received.shape
    step = REACH
    width = table.shape[1]
    rows = n_tm * 8
    chunks = width // (2 * LANES)
    return pl.pallas_call(
        spectra_kernel,
        grid=(slots // step,),
        in_specs=[
            pl.BlockSpec(
                (n_tm, n_chan, 8 * step, lanes), lambda t: (0, 0, first // step + t, 0)
            ),
            pl.BlockSpec(table.shape, lambda t: (0, 0), pipeline_mode=pl.Buffered(1)),
            pl.BlockSpec(memory_space=pl.ANY),
        ],
        out_specs=pl.BlockSpec((2, chunks, step, rows, LANES), lambda t: (0, 0, t, 0, 0)),
        out_shape=pltpu.HBM((2, chunks, slots, rows, LANES), jnp.bfloat16),
        compiler_params=pltpu.CompilerParams(vmem_limit_bytes=32 * MIB),
        cost_estimate=pl.CostEstimate(
            flops=16 * slots * n_tm * width * width,
            bytes_accessed=64 * slots * n_tm * width,
            transcendentals=0,
        ),
        name="delay_spectra",
    )(in_hbm(received.reshape(n_tm, n_chan, pairs, lanes)), in_hbm(table), earlier)


def fold_rows(sums):
    row = lax.broadcasted_iota(jnp.int32, sums[0].shape, 0)
    for bit in (1, 2, 4):
        low = (row & bit) == 0
        merged = []
        for i in range(0, len(sums), 2):
            a, b = sums[i], sums[i + 1]
            kept, moved = jnp.where(low, a, b), jnp.where(low, b, a)
            merged.append(kept + pltpu.roll(moved, 8 - bit, 0))
        sums = merged
    return sums[0]


def cross_tile(rows_ref, s, offsets):
    spans = [pl.ds(8 * g, 8) for g in range(rows_ref.shape[1] // 8)]
    own = [rows_ref[s, span] for span in spans]
    sums = []
    for k in range(1, REACH + 1):
        if k not in offsets:
            sums.append(jnp.zeros((8, LANES), jnp.float32))
            continue
        total = None
        for g, span in enumerate(spans):
            term = own[g] * rows_ref[s + k, span]
            total = term if total is None else total + term
        sums.append(total)
    return fold_rows(sums)


def load_rows(target, at, source):
    target[pl.ds(at, source.shape[0])] = source[...].astype(jnp.float32)


def outer_kernel(head, tail, out_ref, rows_ref):
    load_rows(rows_ref, 0, head.at[0, 0])
    load_rows(rows_ref, REACH, tail.at[0, 0])

    def one_run(i, carry):
        for j in range(REACH):
            s = i * REACH + j
            out_ref[0, s] = cross_tile(rows_ref, s, range(1, REACH - j))
        return carry

    lax.fori_loop(0, 2, one_run, 0)


def inner_kernel(head, inner, tail, out_ref, rows_ref):
    load_rows(rows_ref, 0, head.at[0, 0])
    load_rows(rows_ref, REACH, inner.at[0, 0])
    load_rows(rows_ref, 3 * REACH, tail.at[0, 0])
    for s in range(3 * REACH):
        out_ref[0, s] = cross_tile(rows_ref, s, range(max(1, REACH - s), REACH + 1))


def final_kernel(before, head, tail, after, outer_ref, inner_ref, valid_ref, out_ref, rows_ref):
    shape = (REACH, LANES)
    lane = lax.broadcasted_iota(jnp.int32, shape, 1)
    row = lax.broadcasted_iota(jnp.int32, shape, 0)
    mirror = pl.program_id(0) == 1
    order = jnp.where(mirror, (LANES - lane) % LANES, lane)
    slots = out_ref.shape[0]
    for i, source in enumerate((before, head, tail, after)):
        load_rows(rows_ref, i * REACH, source.at[0, 0])
    powers = {}
    for s in range(-REACH, slots):
        terms = []
        if s < 0 or s >= slots - REACH:
            j = s % REACH
            at = j if s < 0 else 2 * REACH + j
            terms.append(cross_tile(rows_ref, at, range(REACH - j, REACH + 1)))
        if s in OUTER:
            terms.append(outer_ref[0, OUTER.index(s)])
        if 0 <= s < slots - REACH:
            terms.append(inner_ref[0, s])
        value = jnp.take_along_axis(sum(terms[1:], terms[0]), order, axis=1)
        powers[s] = jnp.where(valid_ref[s + REACH] > 0.0, value * (1.0 / 64.0), 0.0)
        if s >= 0:
            out_ref[s, pl.ds(0, REACH), :] = powers[s]
            backward = powers[s - 1]
            for k in range(2, REACH + 1):
                backward = jnp.where(row == k - 1, powers[s - k], backward)
            out_ref[s, pl.ds(REACH, REACH), :] = backward


CHUNKS = 4


def cross_call(kernel, name, operands, specs, out_specs, out_shape, held, pairs):
    rows = 128
    return pl.pallas_call(
        kernel,
        grid=(2, CHUNKS),
        in_specs=specs,
        out_specs=out_specs,
        out_shape=out_shape,
        scratch_shapes=[pltpu.VMEM((held, rows, LANES), jnp.float32)],
        compiler_params=pltpu.CompilerParams(vmem_limit_bytes=24 * MIB),
        cost_estimate=pl.CostEstimate(
            flops=2 * pairs * rows * 1024,
            bytes_accessed=2 * held * rows * 1024,
            transcendentals=0,
        ),
        name=name,
    )(*operands)


def spectra_spec(array):
    return pl.BlockSpec((1, 1) + array.shape[2:], lambda i, j: (i, j, 0, 0, 0))


def sums_spec(slots):
    return pl.BlockSpec((1, slots, REACH, LANES), lambda i, j: (i * CHUNKS + j, 0, 0, 0))


def outer_powers(head, tail):
    slots = 2 * REACH
    return cross_call(
        outer_kernel,
        "outer_pairs",
        [in_hbm(head), in_hbm(tail)],
        [spectra_spec(head)] * 2,
        sums_spec(slots),
        jax.ShapeDtypeStruct((2 * CHUNKS, slots, REACH, LANES), jnp.float32),
        slots,
        56,
    )


def inner_powers(head, inner, tail):
    slots = 3 * REACH
    return cross_call(
        inner_kernel,
        "inner_pairs",
        [in_hbm(head), in_hbm(inner), in_hbm(tail)],
        [spectra_spec(array) for array in (head, inner, tail)],
        sums_spec(slots),
        jax.ShapeDtypeStruct((2 * CHUNKS, slots, REACH, LANES), jnp.float32),
        4 * REACH,
        164,
    )


def final_powers(before, head, tail, after, outer_sums, inner_sums, valid):
    slots = 4 * REACH
    spectra_specs = [spectra_spec(array) for array in (before, head, tail, after)]
    return cross_call(
        final_kernel,
        "pair_power",
        [before, in_hbm(head), in_hbm(tail), after, outer_sums, inner_sums, valid],
        spectra_specs
        + [
            sums_spec(outer_sums.shape[1]),
            sums_spec(inner_sums.shape[1]),
            pl.BlockSpec(valid.shape, lambda i, j: (0, 0, 0)),
        ],
        pl.BlockSpec(
            (slots, 2 * REACH, LANES),
            lambda i, j: (0, 0, jnp.where(i == 0, j, 2 * CHUNKS - 1 - j)),
        ),
        jax.ShapeDtypeStruct((slots, 2 * REACH, 2 * CHUNKS * LANES), jnp.float32),
        slots,
        72,
    )


def body(visibilities, owner_order, group_ids, partner_flags):
    n_tm = lax.axis_size("tm")
    n_chan = lax.axis_size("chan")
    n_dev = n_tm * n_chan
    count, n_base, _, width = visibilities.shape
    per = n_base // n_dev

    table = half_table(width * n_chan)

    start = lax.axis_index(AXES) * per
    groups = lax.dynamic_slice_in_dim(
        jnp.pad(group_ids, (REACH, REACH), constant_values=-1), start, per + 2 * REACH, 0
    )
    flags = lax.dynamic_slice_in_dim(
        jnp.pad(partner_flags, ((REACH, REACH), (0, 0))), start, per + REACH, 0
    )
    own_group = groups[: per + REACH]
    same = jnp.stack([groups[k : k + per + REACH] == own_group for k in range(1, REACH + 1)], 1)
    valid = jnp.broadcast_to(
        (same & (flags == 1)).astype(jnp.float32)[:, :, None], (per + REACH, REACH, LANES)
    )

    def exchange(slots, earlier):
        send = gather(visibilities, owner_order, slots, n_dev, earlier)
        send = send.reshape(n_dev, 2 * count * len(slots), width)
        return lax.all_to_all(send, AXES, 0, 0, tiled=True)

    up = [(i, i + 1) for i in range(n_dev - 1)]
    down = [(i + 1, i) for i in range(n_dev - 1)]
    received_outer = exchange(OUTER, group_ids)
    received_inner = exchange(INNER, table)
    head = spectra(received_outer, table, n_tm, n_chan, 0, REACH, group_ids)
    tail = spectra(received_outer, table, n_tm, n_chan, REACH, REACH, group_ids)
    after = lax.ppermute(head, AXES, down)
    before = lax.ppermute(tail, AXES, up)
    outer_sums = outer_powers(head, tail)
    inner = spectra(received_inner, table, n_tm, n_chan, 0, 2 * REACH, outer_sums)
    inner_sums = inner_powers(head, inner, tail)
    return final_powers(before, head, tail, after, outer_sums, inner_sums, valid)


def solution(mesh):
    return jax.shard_map(
        body,
        mesh=mesh,
        in_specs=(P("tm", None, None, "chan"), P(), P(), P()),
        out_specs=P(AXES, None, None),
        check_vma=False,
    )
```

```python
import functools
import math

import jax
import jax.numpy as jnp
from jax import lax
from jax.experimental import pallas as pl
from jax.experimental.pallas import tpu as pltpu
from jax.sharding import PartitionSpec as P

AXES = ("tm", "chan")
MIB = 2**20
LANES = 128
REACH = 8
OUTER = tuple(range(8)) + tuple(range(24, 32))
INNER = tuple(range(8, 24))


def in_hbm(array):
    return pltpu.with_memory_space_constraint(array, pltpu.HBM)


def half_table(n_chan):
    channel_index = jnp.arange(n_chan, dtype=jnp.int32)
    place = jnp.arange(n_chan, dtype=jnp.int32)
    delay_index = place // (2 * LANES) * LANES + place % LANES
    is_sine = place % (2 * LANES) >= LANES
    middle = is_sine & (delay_index == 0)
    delay_index = jnp.where(middle, n_chan // 2, delay_index)
    turn = jnp.where(is_sine & ~middle, 3 * n_chan // 4, 0)
    phase_index = (channel_index[:, None] * delay_index[None, :] + turn[None, :]) % n_chan
    phase_angle = 2.0 * math.pi / n_chan * phase_index.astype(jnp.float32)
    base_angle = 2.0 * math.pi / n_chan * channel_index.astype(jnp.float32)
    window_taper = (
        0.35875
        - 0.48829 * jnp.cos(base_angle)
        + 0.14128 * jnp.cos(2.0 * base_angle)
        - 0.01168 * jnp.cos(3.0 * base_angle)
    )
    weights_norm = window_taper / jnp.sqrt(jnp.sum(window_taper * window_taper))
    return (weights_norm[:, None] * jnp.cos(phase_angle)).astype(jnp.bfloat16)


def gather_kernel(slots, per, order_ref, vis_ref, _, out_ref):
    owners, count = out_ref.shape[0], out_ref.shape[2]
    first = pl.program_id(0) * owners

    def one_owner(owner, carry):
        base = (first + owner) * per
        for j, slot in enumerate(slots):
            source = order_ref[base + slot]
            for t in range(count):
                out_ref[owner, j, t] = vis_ref[t, source]
        return carry

    lax.fori_loop(0, owners, one_owner, 0)


def gather(visibilities, order, slots, n_dev, earlier):
    count, n_base = visibilities.shape[:2]
    tail = visibilities.shape[2:]
    steps = 8
    return pl.pallas_call(
        functools.partial(gather_kernel, slots, n_base // n_dev),
        grid_spec=pltpu.PrefetchScalarGridSpec(
            num_scalar_prefetch=1,
            grid=(steps,),
            in_specs=[
                pl.BlockSpec(memory_space=pltpu.VMEM),
                pl.BlockSpec(memory_space=pl.ANY),
            ],
            out_specs=pl.BlockSpec(
                (n_dev // steps, len(slots), count) + tail, lambda i, o: (i, 0, 0, 0, 0)
            ),
        ),
        out_shape=pltpu.HBM((n_dev, len(slots), count) + tail, visibilities.dtype),
        compiler_params=pltpu.CompilerParams(vmem_limit_bytes=24 * MIB),
        cost_estimate=pl.CostEstimate(
            flops=0, bytes_accessed=2 * count * n_dev * len(slots) * 512, transcendentals=0
        ),
        name="slot_gather",
    )(in_hbm(order), visibilities, in_hbm(earlier))


def spectra_kernel(received_ref, table_ref, _, out_ref):
    sources, n_chan, rows = received_ref.shape[:3]
    slots = out_ref.shape[2]
    n_rows = sources * rows
    block = jnp.concatenate(
        [received_ref[:, c].reshape(n_rows, LANES) for c in range(n_chan)], axis=1
    )
    chunks = table_ref.shape[1] // (2 * LANES)
    shape = (n_rows // 8, 8, LANES)
    first = lax.broadcasted_iota(jnp.int32, shape, 2) == 0
    is_real = lax.broadcasted_iota(jnp.int32, shape, 1) % 2 == 0

    def store(sign, c, value):
        value = jnp.swapaxes(value.reshape(sources, slots, 8, LANES), 0, 1)
        value = value.reshape(slots, sources * 8, LANES).astype(jnp.bfloat16)
        out_ref[sign, c] = value

    minus = []
    for c in range(chunks):
        both = jnp.dot(
            block, table_ref[:, pl.ds(2 * c * LANES, 2 * LANES)], preferred_element_type=jnp.float32
        )
        cosine, sine = both[:, :LANES].reshape(shape), both[:, LANES:].reshape(shape)
        other = jnp.where(is_real, pltpu.roll(sine, 7, 1), -pltpu.roll(sine, 1, 1))
        ahead, back = cosine + other, cosine - other
        if c == 0:
            ahead, back = jnp.where(first, cosine, ahead), jnp.where(first, sine, back)
        store(0, c, ahead)
        minus.append(back)
        if c > 0:
            store(1, c - 1, jnp.where(first, back, minus[c - 1]))
    store(1, chunks - 1, jnp.where(first, minus[0], minus[-1]))


def spectra(received, table, n_tm, n_chan, first, slots, earlier):
    _, pairs, lanes = received.shape
    step = REACH
    width = table.shape[1]
    rows = n_tm * 8
    chunks = width // (2 * LANES)
    return pl.pallas_call(
        spectra_kernel,
        grid=(slots // step,),
        in_specs=[
            pl.BlockSpec(
                (n_tm, n_chan, 8 * step, lanes), lambda t: (0, 0, first // step + t, 0)
            ),
            pl.BlockSpec(table.shape, lambda t: (0, 0), pipeline_mode=pl.Buffered(1)),
            pl.BlockSpec(memory_space=pl.ANY),
        ],
        out_specs=pl.BlockSpec((2, chunks, step, rows, LANES), lambda t: (0, 0, t, 0, 0)),
        out_shape=pltpu.HBM((2, chunks, slots, rows, LANES), jnp.bfloat16),
        compiler_params=pltpu.CompilerParams(vmem_limit_bytes=32 * MIB),
        cost_estimate=pl.CostEstimate(
            flops=16 * slots * n_tm * width * width,
            bytes_accessed=64 * slots * n_tm * width,
            transcendentals=0,
        ),
        name="delay_spectra",
    )(in_hbm(received.reshape(n_tm, n_chan, pairs, lanes)), in_hbm(table), earlier)


def fold_rows(sums):
    row = lax.broadcasted_iota(jnp.int32, sums[0].shape, 0)
    for bit in (1, 2, 4):
        low = (row & bit) == 0
        merged = []
        for i in range(0, len(sums), 2):
            a, b = sums[i], sums[i + 1]
            kept, moved = jnp.where(low, a, b), jnp.where(low, b, a)
            merged.append(kept + pltpu.roll(moved, 8 - bit, 0))
        sums = merged
    return sums[0]


def cross_tile(rows_ref, s, offsets):
    spans = [pl.ds(8 * g, 8) for g in range(rows_ref.shape[1] // 8)]
    own = [rows_ref[s, span] for span in spans]
    sums = []
    for k in range(1, REACH + 1):
        if k not in offsets:
            sums.append(jnp.zeros((8, LANES), jnp.float32))
            continue
        total = None
        for g, span in enumerate(spans):
            term = own[g] * rows_ref[s + k, span]
            total = term if total is None else total + term
        sums.append(total)
    return fold_rows(sums)


def load_rows(target, at, source):
    target[pl.ds(at, source.shape[0])] = source[...].astype(jnp.float32)


def outer_kernel(head, tail, out_ref, rows_ref):
    load_rows(rows_ref, 0, head.at[0, 0])
    load_rows(rows_ref, REACH, tail.at[0, 0])

    def one_run(i, carry):
        for j in range(REACH):
            s = i * REACH + j
            out_ref[0, s] = cross_tile(rows_ref, s, range(1, REACH - j))
        return carry

    lax.fori_loop(0, 2, one_run, 0)


def edge_kernel(tail, after, before, head, _, next_ref, prev_ref, rows_ref):
    for left, right, out_ref in ((tail, after, next_ref), (before, head, prev_ref)):
        load_rows(rows_ref, 0, left.at[0, 0])
        load_rows(rows_ref, REACH, right.at[0, 0])
        for j in range(REACH):
            out_ref[0, j] = cross_tile(rows_ref, j, range(REACH - j, REACH + 1))


def final_kernel(
    head, inner, tail, outer_ref, next_a, next_b, prev_a, prev_b, valid_ref, out_ref, rows_ref
):
    shape = (REACH, LANES)
    lane = lax.broadcasted_iota(jnp.int32, shape, 1)
    row = lax.broadcasted_iota(jnp.int32, shape, 0)
    mirror = pl.program_id(0) == 1
    order = jnp.where(mirror, (LANES - lane) % LANES, lane)
    slots = out_ref.shape[0]
    load_rows(rows_ref, 0, head.at[0, 0])
    load_rows(rows_ref, REACH, inner.at[0, 0])
    load_rows(rows_ref, 3 * REACH, tail.at[0, 0])
    powers = {}
    for s in range(-REACH, slots):
        terms = []
        if s < 0:
            terms += [prev_a[0, s + REACH], prev_b[0, s + REACH]]
        if s in OUTER:
            terms.append(outer_ref[0, OUTER.index(s)])
        if 0 <= s < slots - REACH:
            terms.append(cross_tile(rows_ref, s, range(max(1, REACH - s), REACH + 1)))
        if s >= slots - REACH:
            j = s - (slots - REACH)
            terms += [next_a[0, j], next_b[0, j]]
        value = jnp.take_along_axis(sum(terms[1:], terms[0]), order, axis=1)
        powers[s] = jnp.where(valid_ref[s + REACH] > 0.0, value * (1.0 / 64.0), 0.0)
        if s >= 0:
            out_ref[s, pl.ds(0, REACH), :] = powers[s]
            backward = powers[s - 1]
            for k in range(2, REACH + 1):
                backward = jnp.where(row == k - 1, powers[s - k], backward)
            out_ref[s, pl.ds(REACH, REACH), :] = backward


CHUNKS = 4


def cross_call(kernel, name, operands, specs, out_specs, out_shape, held, pairs, rows=128):
    return pl.pallas_call(
        kernel,
        grid=(2, CHUNKS),
        in_specs=specs,
        out_specs=out_specs,
        out_shape=out_shape,
        scratch_shapes=[pltpu.VMEM((held, rows, LANES), jnp.float32)],
        compiler_params=pltpu.CompilerParams(vmem_limit_bytes=24 * MIB),
        cost_estimate=pl.CostEstimate(
            flops=2 * pairs * rows * 1024,
            bytes_accessed=2 * held * rows * 1024,
            transcendentals=0,
        ),
        name=name,
    )(*operands)


def spectra_spec(array):
    return pl.BlockSpec((1, 1) + array.shape[2:], lambda i, j: (i, j, 0, 0, 0))


def sums_spec(slots):
    return pl.BlockSpec((1, slots, REACH, LANES), lambda i, j: (i * CHUNKS + j, 0, 0, 0))


def outer_powers(head, tail):
    slots = 2 * REACH
    return cross_call(
        outer_kernel,
        "outer_pairs",
        [in_hbm(head), in_hbm(tail)],
        [spectra_spec(head)] * 2,
        sums_spec(slots),
        jax.ShapeDtypeStruct((2 * CHUNKS, slots, REACH, LANES), jnp.float32),
        slots,
        56,
    )


def edge_powers(tail, after, before, head, earlier):
    rows = after.shape[3]
    shape = jax.ShapeDtypeStruct((2 * CHUNKS, REACH, REACH, LANES), jnp.float32)

    def half(which):
        return pl.BlockSpec((1, 1, REACH, rows, LANES), lambda i, j: (i, j, 0, which, 0))

    return cross_call(
        edge_kernel,
        "edge_pairs",
        [in_hbm(tail), in_hbm(after), in_hbm(before), in_hbm(head), earlier],
        [half(0), half(0), half(0), half(1), pl.BlockSpec(memory_space=pl.ANY)],
        [sums_spec(REACH)] * 2,
        [shape, shape],
        2 * REACH,
        36 * 100000,
        rows,
    )


def final_powers(head, inner, tail, outer_sums, following, preceding, valid):
    slots = 4 * REACH
    edges = [*following, *preceding]
    return cross_call(
        final_kernel,
        "pair_power",
        [in_hbm(head), in_hbm(inner), in_hbm(tail), outer_sums, *edges, valid],
        [spectra_spec(array) for array in (head, inner, tail)]
        + [sums_spec(outer_sums.shape[1])]
        + [sums_spec(REACH)] * len(edges)
        + [pl.BlockSpec(valid.shape, lambda i, j: (0, 0, 0))],
        pl.BlockSpec(
            (slots, 2 * REACH, LANES),
            lambda i, j: (0, 0, jnp.where(i == 0, j, 2 * CHUNKS - 1 - j)),
        ),
        jax.ShapeDtypeStruct((slots, 2 * REACH, 2 * CHUNKS * LANES), jnp.float32),
        slots,
        164,
    )


def edge_rows_kernel(received, _, head, tail, __, sems):
    near, edge = head.shape[:2]
    copies = [
        pltpu.make_async_copy(received.at[pl.ds(0, near), pl.ds(0, edge)], head, sems.at[0]),
        pltpu.make_async_copy(received.at[pl.ds(near, near), pl.ds(edge, edge)], tail, sems.at[1]),
    ]
    for copy in copies:
        copy.start()
    for copy in copies:
        copy.wait()


def edge_rows(received, send):
    sources, rows, lanes = received.shape
    part = pltpu.HBM((sources // 2, rows // 2, lanes), received.dtype)
    anywhere = pl.BlockSpec(memory_space=pl.ANY)
    return pl.pallas_call(
        edge_rows_kernel,
        in_specs=[anywhere] * 2,
        out_specs=[anywhere] * 3,
        out_shape=[part, part, pltpu.HBM(send.shape, send.dtype)],
        scratch_shapes=[pltpu.SemaphoreType.DMA((2,))],
        input_output_aliases={1: 2},
        name="edge_rows",
    )(in_hbm(received), in_hbm(send))


def body(visibilities, owner_order, group_ids, partner_flags):
    n_tm = lax.axis_size("tm")
    n_chan = lax.axis_size("chan")
    n_dev = n_tm * n_chan
    count, n_base, _, width = visibilities.shape
    per = n_base // n_dev

    table = half_table(width * n_chan)

    start = lax.axis_index(AXES) * per
    groups = lax.dynamic_slice_in_dim(
        jnp.pad(group_ids, (REACH, REACH), constant_values=-1), start, per + 2 * REACH, 0
    )
    flags = lax.dynamic_slice_in_dim(
        jnp.pad(partner_flags, ((REACH, REACH), (0, 0))), start, per + REACH, 0
    )
    own_group = groups[: per + REACH]
    same = jnp.stack([groups[k : k + per + REACH] == own_group for k in range(1, REACH + 1)], 1)
    valid = jnp.broadcast_to(
        (same & (flags == 1)).astype(jnp.float32)[:, :, None], (per + REACH, REACH, LANES)
    )

    def rows_for_owners(slots, earlier):
        send = gather(visibilities, owner_order, slots, n_dev, earlier)
        return send.reshape(n_dev, 2 * count * len(slots), width)

    def exchange(send):
        return lax.all_to_all(send, AXES, 0, 0, tiled=True)

    up = [(i, i + 1) for i in range(n_dev - 1)]
    down = [(i + 1, i) for i in range(n_dev - 1)]
    received_outer = exchange(rows_for_owners(OUTER, group_ids))
    send_inner = rows_for_owners(INNER, table)
    head_rows, tail_rows, send_inner = edge_rows(received_outer, send_inner)
    after_rows = lax.ppermute(head_rows, AXES, down)
    before_rows = lax.ppermute(tail_rows, AXES, up)
    received_inner = exchange(send_inner)
    head = spectra(received_outer, table, n_tm, n_chan, 0, REACH, group_ids)
    tail = spectra(received_outer, table, n_tm, n_chan, REACH, REACH, group_ids)
    outer_sums = outer_powers(head, tail)
    after = spectra(after_rows, table, n_tm // 2, n_chan, 0, REACH, outer_sums)
    before = spectra(before_rows, table, n_tm // 2, n_chan, 0, REACH, outer_sums)
    next_sums, prev_sums = edge_powers(tail, after, before, head, outer_sums)
    prev_other = lax.ppermute(next_sums, AXES, up)
    next_other = lax.ppermute(prev_sums, AXES, down)
    inner = spectra(received_inner, table, n_tm, n_chan, 0, 2 * REACH, next_sums)
    return final_powers(
        head, inner, tail, outer_sums, (next_sums, next_other), (prev_sums, prev_other), valid
    )


def solution(mesh):
    return jax.shard_map(
        body,
        mesh=mesh,
        in_specs=(P("tm", None, None, "chan"), P(), P(), P()),
        out_specs=P(AXES, None, None),
        check_vma=False,
    )
```

```python
import functools
import math

import jax
import jax.numpy as jnp
from jax import lax
from jax.experimental import pallas as pl
from jax.experimental.pallas import tpu as pltpu
from jax.sharding import PartitionSpec as P

AXES = ("tm", "chan")
MIB = 2**20
LANES = 128
REACH = 8
OUTER = tuple(range(8)) + tuple(range(24, 32))
INNER = tuple(range(8, 24))


def in_hbm(array):
    return pltpu.with_memory_space_constraint(array, pltpu.HBM)


def half_table(n_chan):
    channel_index = jnp.arange(n_chan, dtype=jnp.int32)
    place = jnp.arange(n_chan, dtype=jnp.int32)
    delay_index = place // (2 * LANES) * LANES + place % LANES
    is_sine = place % (2 * LANES) >= LANES
    middle = is_sine & (delay_index == 0)
    delay_index = jnp.where(middle, n_chan // 2, delay_index)
    turn = jnp.where(is_sine & ~middle, 3 * n_chan // 4, 0)
    phase_index = (channel_index[:, None] * delay_index[None, :] + turn[None, :]) % n_chan
    phase_angle = 2.0 * math.pi / n_chan * phase_index.astype(jnp.float32)
    base_angle = 2.0 * math.pi / n_chan * channel_index.astype(jnp.float32)
    window_taper = (
        0.35875
        - 0.48829 * jnp.cos(base_angle)
        + 0.14128 * jnp.cos(2.0 * base_angle)
        - 0.01168 * jnp.cos(3.0 * base_angle)
    )
    weights_norm = window_taper / jnp.sqrt(jnp.sum(window_taper * window_taper))
    return (weights_norm[:, None] * jnp.cos(phase_angle)).astype(jnp.bfloat16)


def gather_kernel(slots, per, order_ref, vis_ref, _, out_ref):
    owners, count = out_ref.shape[0], out_ref.shape[2]
    first = pl.program_id(0) * owners

    def one_owner(owner, carry):
        base = (first + owner) * per
        for j, slot in enumerate(slots):
            source = order_ref[base + slot]
            for t in range(count):
                out_ref[owner, j, t] = vis_ref[t, source]
        return carry

    lax.fori_loop(0, owners, one_owner, 0)


def gather(visibilities, order, slots, n_dev, earlier):
    count, n_base = visibilities.shape[:2]
    tail = visibilities.shape[2:]
    steps = 8
    return pl.pallas_call(
        functools.partial(gather_kernel, slots, n_base // n_dev),
        grid_spec=pltpu.PrefetchScalarGridSpec(
            num_scalar_prefetch=1,
            grid=(steps,),
            in_specs=[
                pl.BlockSpec(memory_space=pltpu.VMEM),
                pl.BlockSpec(memory_space=pl.ANY),
            ],
            out_specs=pl.BlockSpec(
                (n_dev // steps, len(slots), count) + tail, lambda i, o: (i, 0, 0, 0, 0)
            ),
        ),
        out_shape=pltpu.HBM((n_dev, len(slots), count) + tail, visibilities.dtype),
        compiler_params=pltpu.CompilerParams(vmem_limit_bytes=24 * MIB),
        cost_estimate=pl.CostEstimate(
            flops=0, bytes_accessed=2 * count * n_dev * len(slots) * 512, transcendentals=0
        ),
        name="slot_gather",
    )(in_hbm(order), visibilities, in_hbm(earlier))


def spectra_kernel(received_ref, table_ref, _, out_ref):
    sources, n_chan, rows = received_ref.shape[:3]
    slots = out_ref.shape[2]
    n_rows = sources * rows
    block = jnp.concatenate(
        [received_ref[:, c].reshape(n_rows, LANES) for c in range(n_chan)], axis=1
    )
    chunks = table_ref.shape[1] // (2 * LANES)
    shape = (n_rows // 8, 8, LANES)
    first = lax.broadcasted_iota(jnp.int32, shape, 2) == 0
    is_real = lax.broadcasted_iota(jnp.int32, shape, 1) % 2 == 0

    def store(sign, c, value):
        value = jnp.swapaxes(value.reshape(sources, slots, 8, LANES), 0, 1)
        value = value.reshape(slots, sources * 8, LANES).astype(jnp.bfloat16)
        out_ref[sign, c] = value

    minus = []
    for c in range(chunks):
        both = jnp.dot(
            block, table_ref[:, pl.ds(2 * c * LANES, 2 * LANES)], preferred_element_type=jnp.float32
        )
        cosine, sine = both[:, :LANES].reshape(shape), both[:, LANES:].reshape(shape)
        other = jnp.where(is_real, pltpu.roll(sine, 7, 1), -pltpu.roll(sine, 1, 1))
        ahead, back = cosine + other, cosine - other
        if c == 0:
            ahead, back = jnp.where(first, cosine, ahead), jnp.where(first, sine, back)
        store(0, c, ahead)
        minus.append(back)
        if c > 0:
            store(1, c - 1, jnp.where(first, back, minus[c - 1]))
    store(1, chunks - 1, jnp.where(first, minus[0], minus[-1]))


def spectra(received, table, n_tm, n_chan, first, slots, earlier):
    _, pairs, lanes = received.shape
    step = REACH
    width = table.shape[1]
    rows = n_tm * 8
    chunks = width // (2 * LANES)
    return pl.pallas_call(
        spectra_kernel,
        grid=(slots // step,),
        in_specs=[
            pl.BlockSpec(
                (n_tm, n_chan, 8 * step, lanes), lambda t: (0, 0, first // step + t, 0)
            ),
            pl.BlockSpec(table.shape, lambda t: (0, 0), pipeline_mode=pl.Buffered(1)),
            pl.BlockSpec(memory_space=pl.ANY),
        ],
        out_specs=pl.BlockSpec((2, chunks, step, rows, LANES), lambda t: (0, 0, t, 0, 0)),
        out_shape=pltpu.HBM((2, chunks, slots, rows, LANES), jnp.bfloat16),
        compiler_params=pltpu.CompilerParams(vmem_limit_bytes=32 * MIB),
        cost_estimate=pl.CostEstimate(
            flops=16 * slots * n_tm * width * width,
            bytes_accessed=64 * slots * n_tm * width,
            transcendentals=0,
        ),
        name="delay_spectra",
    )(in_hbm(received.reshape(n_tm, n_chan, pairs, lanes)), in_hbm(table), earlier)


def fold_rows(sums):
    row = lax.broadcasted_iota(jnp.int32, sums[0].shape, 0)
    for bit in (1, 2, 4):
        low = (row & bit) == 0
        merged = []
        for i in range(0, len(sums), 2):
            a, b = sums[i], sums[i + 1]
            kept, moved = jnp.where(low, a, b), jnp.where(low, b, a)
            merged.append(kept + pltpu.roll(moved, 8 - bit, 0))
        sums = merged
    return sums[0]


def cross_tile(rows_ref, s, offsets):
    spans = [pl.ds(8 * g, 8) for g in range(rows_ref.shape[1] // 8)]
    own = [rows_ref[s, span] for span in spans]
    sums = []
    for k in range(1, REACH + 1):
        if k not in offsets:
            sums.append(jnp.zeros((8, LANES), jnp.float32))
            continue
        total = None
        for g, span in enumerate(spans):
            term = own[g] * rows_ref[s + k, span]
            total = term if total is None else total + term
        sums.append(total)
    return fold_rows(sums)


def load_rows(target, at, source):
    target[pl.ds(at, source.shape[0])] = source[...].astype(jnp.float32)


def outer_kernel(head, tail, out_ref, rows_ref):
    load_rows(rows_ref, 0, head.at[0, 0])
    load_rows(rows_ref, REACH, tail.at[0, 0])

    def one_run(i, carry):
        for j in range(REACH):
            s = i * REACH + j
            out_ref[0, s] = cross_tile(rows_ref, s, range(1, REACH - j))
        return carry

    lax.fori_loop(0, 2, one_run, 0)


def inner_kernel(head, inner, tail, out_ref, rows_ref):
    load_rows(rows_ref, 0, head.at[0, 0])
    load_rows(rows_ref, REACH, inner.at[0, 0])
    load_rows(rows_ref, 3 * REACH, tail.at[0, 0])
    for s in range(3 * REACH):
        out_ref[0, s] = cross_tile(rows_ref, s, range(max(1, REACH - s), REACH + 1))


def final_kernel(before, head, tail, after, outer_ref, inner_ref, valid_ref, out_ref, rows_ref):
    shape = (REACH, LANES)
    lane = lax.broadcasted_iota(jnp.int32, shape, 1)
    row = lax.broadcasted_iota(jnp.int32, shape, 0)
    mirror = pl.program_id(0) == 1
    order = jnp.where(mirror, (LANES - lane) % LANES, lane)
    slots = out_ref.shape[0]
    for i, source in enumerate((before, head, tail, after)):
        load_rows(rows_ref, i * REACH, source.at[0, 0])
    powers = {}
    for s in range(-REACH, slots):
        terms = []
        if s < 0 or s >= slots - REACH:
            j = s % REACH
            at = j if s < 0 else 2 * REACH + j
            terms.append(cross_tile(rows_ref, at, range(REACH - j, REACH + 1)))
        if s in OUTER:
            terms.append(outer_ref[0, OUTER.index(s)])
        if 0 <= s < slots - REACH:
            terms.append(inner_ref[0, s])
        value = jnp.take_along_axis(sum(terms[1:], terms[0]), order, axis=1)
        powers[s] = jnp.where(valid_ref[s + REACH] > 0.0, value * (1.0 / 64.0), 0.0)
        if s >= 0:
            out_ref[s, pl.ds(0, REACH), :] = powers[s]
            backward = powers[s - 1]
            for k in range(2, REACH + 1):
                backward = jnp.where(row == k - 1, powers[s - k], backward)
            out_ref[s, pl.ds(REACH, REACH), :] = backward


CHUNKS = 4


def cross_call(kernel, name, operands, specs, out_specs, out_shape, held, pairs):
    rows = 128
    return pl.pallas_call(
        kernel,
        grid=(2, CHUNKS),
        in_specs=specs,
        out_specs=out_specs,
        out_shape=out_shape,
        scratch_shapes=[pltpu.VMEM((held, rows, LANES), jnp.float32)],
        compiler_params=pltpu.CompilerParams(vmem_limit_bytes=24 * MIB),
        cost_estimate=pl.CostEstimate(
            flops=2 * pairs * rows * 1024,
            bytes_accessed=2 * held * rows * 1024,
            transcendentals=0,
        ),
        name=name,
    )(*operands)


def spectra_spec(array):
    return pl.BlockSpec((1, 1) + array.shape[2:], lambda i, j: (i, j, 0, 0, 0))


def sums_spec(slots):
    return pl.BlockSpec((1, slots, REACH, LANES), lambda i, j: (i * CHUNKS + j, 0, 0, 0))


def outer_powers(head, tail):
    slots = 2 * REACH
    return cross_call(
        outer_kernel,
        "outer_pairs",
        [in_hbm(head), in_hbm(tail)],
        [spectra_spec(head)] * 2,
        sums_spec(slots),
        jax.ShapeDtypeStruct((2 * CHUNKS, slots, REACH, LANES), jnp.float32),
        slots,
        56,
    )


def inner_powers(head, inner, tail):
    slots = 3 * REACH
    return cross_call(
        inner_kernel,
        "inner_pairs",
        [in_hbm(head), in_hbm(inner), in_hbm(tail)],
        [spectra_spec(array) for array in (head, inner, tail)],
        sums_spec(slots),
        jax.ShapeDtypeStruct((2 * CHUNKS, slots, REACH, LANES), jnp.float32),
        4 * REACH,
        164,
    )


def final_powers(before, head, tail, after, outer_sums, inner_sums, valid):
    slots = 4 * REACH
    spectra_specs = [spectra_spec(array) for array in (before, head, tail, after)]
    return cross_call(
        final_kernel,
        "pair_power",
        [before, in_hbm(head), in_hbm(tail), after, outer_sums, inner_sums, valid],
        spectra_specs
        + [
            sums_spec(outer_sums.shape[1]),
            sums_spec(inner_sums.shape[1]),
            pl.BlockSpec(valid.shape, lambda i, j: (0, 0, 0)),
        ],
        pl.BlockSpec(
            (slots, 2 * REACH, LANES),
            lambda i, j: (0, 0, jnp.where(i == 0, j, 2 * CHUNKS - 1 - j)),
        ),
        jax.ShapeDtypeStruct((slots, 2 * REACH, 2 * CHUNKS * LANES), jnp.float32),
        slots,
        72,
    )


def after_those(arrays, *earlier):
    def kernel(*refs):
        pass

    count = len(arrays)
    anywhere = pl.BlockSpec(memory_space=pl.ANY)
    return pl.pallas_call(
        kernel,
        in_specs=[anywhere] * (count + len(earlier)),
        out_specs=[anywhere] * count,
        out_shape=[pltpu.HBM(array.shape, array.dtype) for array in arrays],
        input_output_aliases={i: i for i in range(count)},
        name="in_order",
    )(*[in_hbm(array) for array in arrays], *earlier)


def body(visibilities, owner_order, group_ids, partner_flags):
    n_tm = lax.axis_size("tm")
    n_chan = lax.axis_size("chan")
    n_dev = n_tm * n_chan
    count, n_base, _, width = visibilities.shape
    per = n_base // n_dev

    table = half_table(width * n_chan)

    start = lax.axis_index(AXES) * per
    groups = lax.dynamic_slice_in_dim(
        jnp.pad(group_ids, (REACH, REACH), constant_values=-1), start, per + 2 * REACH, 0
    )
    flags = lax.dynamic_slice_in_dim(
        jnp.pad(partner_flags, ((REACH, REACH), (0, 0))), start, per + REACH, 0
    )
    own_group = groups[: per + REACH]
    same = jnp.stack([groups[k : k + per + REACH] == own_group for k in range(1, REACH + 1)], 1)
    valid = jnp.broadcast_to(
        (same & (flags == 1)).astype(jnp.float32)[:, :, None], (per + REACH, REACH, LANES)
    )

    def exchange(slots, earlier):
        send = gather(visibilities, owner_order, slots, n_dev, earlier)
        send = send.reshape(n_dev, 2 * count * len(slots), width)
        return lax.all_to_all(send, AXES, 0, 0, tiled=True)

    up = [(i, i + 1) for i in range(n_dev - 1)]
    down = [(i + 1, i) for i in range(n_dev - 1)]
    received_outer = exchange(OUTER, group_ids)
    received_inner = exchange(INNER, group_ids)
    head = spectra(received_outer, table, n_tm, n_chan, 0, REACH, group_ids)
    tail = spectra(received_outer, table, n_tm, n_chan, REACH, REACH, group_ids)
    outer_sums = outer_powers(head, tail)
    head_sent, tail_sent = after_those((head, tail), outer_sums)
    after = lax.ppermute(head_sent, AXES, down)
    before = lax.ppermute(tail_sent, AXES, up)
    inner = spectra(received_inner, table, n_tm, n_chan, 0, 2 * REACH, outer_sums)
    inner_sums = inner_powers(head_sent, inner, tail_sent)
    return final_powers(before, head_sent, tail_sent, after, outer_sums, inner_sums, valid)


def solution(mesh):
    return jax.shard_map(
        body,
        mesh=mesh,
        in_specs=(P("tm", None, None, "chan"), P(), P(), P()),
        out_specs=P(AXES, None, None),
        check_vma=False,
    )
```

```python
import functools
import math

import jax
import jax.numpy as jnp
from jax import lax
from jax.experimental import pallas as pl
from jax.experimental.pallas import tpu as pltpu
from jax.sharding import PartitionSpec as P

AXES = ("tm", "chan")
MIB = 2**20
LANES = 128
REACH = 8
HEAD, TAIL = tuple(range(8)), tuple(range(24, 32))
MIDDLE = tuple(range(8, 12)) + tuple(range(20, 24))
OUTER = HEAD + MIDDLE + TAIL
INNER = tuple(range(12, 20))


def in_hbm(array):
    return pltpu.with_memory_space_constraint(array, pltpu.HBM)


def half_table(n_chan):
    channel_index = jnp.arange(n_chan, dtype=jnp.int32)
    place = jnp.arange(n_chan, dtype=jnp.int32)
    delay_index = place // (2 * LANES) * LANES + place % LANES
    is_sine = place % (2 * LANES) >= LANES
    middle = is_sine & (delay_index == 0)
    delay_index = jnp.where(middle, n_chan // 2, delay_index)
    turn = jnp.where(is_sine & ~middle, 3 * n_chan // 4, 0)
    phase_index = (channel_index[:, None] * delay_index[None, :] + turn[None, :]) % n_chan
    phase_angle = 2.0 * math.pi / n_chan * phase_index.astype(jnp.float32)
    base_angle = 2.0 * math.pi / n_chan * channel_index.astype(jnp.float32)
    window_taper = (
        0.35875
        - 0.48829 * jnp.cos(base_angle)
        + 0.14128 * jnp.cos(2.0 * base_angle)
        - 0.01168 * jnp.cos(3.0 * base_angle)
    )
    weights_norm = window_taper / jnp.sqrt(jnp.sum(window_taper * window_taper))
    return (weights_norm[:, None] * jnp.cos(phase_angle)).astype(jnp.bfloat16)


def gather_kernel(slots, per, order_ref, vis_ref, _, out_ref):
    owners, count = out_ref.shape[0], out_ref.shape[2]
    first = pl.program_id(0) * owners

    def one_owner(owner, carry):
        base = (first + owner) * per
        for j, slot in enumerate(slots):
            source = order_ref[base + slot]
            for t in range(count):
                out_ref[owner, j, t] = vis_ref[t, source]
        return carry

    lax.fori_loop(0, owners, one_owner, 0)


def gather(visibilities, order, slots, n_dev, earlier):
    count, n_base = visibilities.shape[:2]
    tail = visibilities.shape[2:]
    steps = 8
    return pl.pallas_call(
        functools.partial(gather_kernel, slots, n_base // n_dev),
        grid_spec=pltpu.PrefetchScalarGridSpec(
            num_scalar_prefetch=1,
            grid=(steps,),
            in_specs=[
                pl.BlockSpec(memory_space=pltpu.VMEM),
                pl.BlockSpec(memory_space=pl.ANY),
            ],
            out_specs=pl.BlockSpec(
                (n_dev // steps, len(slots), count) + tail, lambda i, o: (i, 0, 0, 0, 0)
            ),
        ),
        out_shape=pltpu.HBM((n_dev, len(slots), count) + tail, visibilities.dtype),
        compiler_params=pltpu.CompilerParams(vmem_limit_bytes=24 * MIB),
        cost_estimate=pl.CostEstimate(
            flops=0, bytes_accessed=2 * count * n_dev * len(slots) * 512, transcendentals=0
        ),
        name="slot_gather",
    )(in_hbm(order), visibilities, in_hbm(earlier))


def spectra_kernel(received_ref, table_ref, _, out_ref):
    sources, n_chan, rows = received_ref.shape[:3]
    slots = out_ref.shape[2]
    n_rows = sources * rows
    block = jnp.concatenate(
        [received_ref[:, c].reshape(n_rows, LANES) for c in range(n_chan)], axis=1
    )
    chunks = table_ref.shape[1] // (2 * LANES)
    shape = (n_rows // 8, 8, LANES)
    first = lax.broadcasted_iota(jnp.int32, shape, 2) == 0
    is_real = lax.broadcasted_iota(jnp.int32, shape, 1) % 2 == 0

    def store(sign, c, value):
        value = jnp.swapaxes(value.reshape(sources, slots, 8, LANES), 0, 1)
        value = value.reshape(slots, sources * 8, LANES).astype(jnp.bfloat16)
        out_ref[sign, c] = value

    minus = []
    for c in range(chunks):
        both = jnp.dot(
            block, table_ref[:, pl.ds(2 * c * LANES, 2 * LANES)], preferred_element_type=jnp.float32
        )
        cosine, sine = both[:, :LANES].reshape(shape), both[:, LANES:].reshape(shape)
        other = jnp.where(is_real, pltpu.roll(sine, 7, 1), -pltpu.roll(sine, 1, 1))
        ahead, back = cosine + other, cosine - other
        if c == 0:
            ahead, back = jnp.where(first, cosine, ahead), jnp.where(first, sine, back)
        store(0, c, ahead)
        minus.append(back)
        if c > 0:
            store(1, c - 1, jnp.where(first, back, minus[c - 1]))
    store(1, chunks - 1, jnp.where(first, minus[0], minus[-1]))


def spectra(received, table, n_tm, n_chan, first, slots, earlier):
    _, pairs, lanes = received.shape
    step = REACH
    width = table.shape[1]
    rows = n_tm * 8
    chunks = width // (2 * LANES)
    return pl.pallas_call(
        spectra_kernel,
        grid=(slots // step,),
        in_specs=[
            pl.BlockSpec(
                (n_tm, n_chan, 8 * step, lanes), lambda t: (0, 0, first // step + t, 0)
            ),
            pl.BlockSpec(table.shape, lambda t: (0, 0), pipeline_mode=pl.Buffered(1)),
            pl.BlockSpec(memory_space=pl.ANY),
        ],
        out_specs=pl.BlockSpec((2, chunks, step, rows, LANES), lambda t: (0, 0, t, 0, 0)),
        out_shape=pltpu.HBM((2, chunks, slots, rows, LANES), jnp.bfloat16),
        compiler_params=pltpu.CompilerParams(vmem_limit_bytes=32 * MIB),
        cost_estimate=pl.CostEstimate(
            flops=16 * slots * n_tm * width * width,
            bytes_accessed=64 * slots * n_tm * width,
            transcendentals=0,
        ),
        name="delay_spectra",
    )(in_hbm(received.reshape(n_tm, n_chan, pairs, lanes)), in_hbm(table), in_hbm(earlier))


def fold_rows(sums):
    row = lax.broadcasted_iota(jnp.int32, sums[0].shape, 0)
    for bit in (1, 2, 4):
        low = (row & bit) == 0
        merged = []
        for i in range(0, len(sums), 2):
            a, b = sums[i], sums[i + 1]
            kept, moved = jnp.where(low, a, b), jnp.where(low, b, a)
            merged.append(kept + pltpu.roll(moved, 8 - bit, 0))
        sums = merged
    return sums[0]


def cross_tile(rows_ref, s, offsets):
    spans = [pl.ds(8 * g, 8) for g in range(rows_ref.shape[1] // 8)]
    own = [rows_ref[s, span] for span in spans]
    sums = []
    for k in range(1, REACH + 1):
        if k not in offsets:
            sums.append(jnp.zeros((8, LANES), jnp.float32))
            continue
        total = None
        for g, span in enumerate(spans):
            term = own[g] * rows_ref[s + k, span]
            total = term if total is None else total + term
        sums.append(total)
    return fold_rows(sums)


def load_rows(target, at, source):
    target[pl.ds(at, source.shape[0])] = source[...].astype(jnp.float32)


def outer_kernel(head, middle, tail, out_ref, rows_ref):
    load_rows(rows_ref, 0, head.at[0, 0])
    load_rows(rows_ref, REACH, middle.at[0, 0])
    load_rows(rows_ref, 2 * REACH, tail.at[0, 0])
    run = len(OUTER) // 2

    def one_run(i, carry):
        for j in range(run):
            s = i * run + j
            out_ref[0, s] = cross_tile(rows_ref, s, range(1, min(REACH, run - 1 - j) + 1))
        return carry

    lax.fori_loop(0, 2, one_run, 0)


def inner_kernel(head, middle, inner, tail, out_ref, rows_ref):
    load_rows(rows_ref, 0, head.at[0, 0, pl.ds(4, 4)])
    load_rows(rows_ref, 4, middle.at[0, 0, pl.ds(0, 4)])
    load_rows(rows_ref, 8, inner.at[0, 0])
    load_rows(rows_ref, 16, middle.at[0, 0, pl.ds(4, 4)])
    load_rows(rows_ref, 20, tail.at[0, 0, pl.ds(0, 4)])
    for j in range(2 * REACH):
        out_ref[0, j] = cross_tile(rows_ref, j, range(max(1, REACH - j), REACH + 1))


def final_kernel(before, head, tail, after, outer_ref, inner_ref, valid_ref, out_ref, rows_ref):
    shape = (REACH, LANES)
    lane = lax.broadcasted_iota(jnp.int32, shape, 1)
    row = lax.broadcasted_iota(jnp.int32, shape, 0)
    mirror = pl.program_id(0) == 1
    order = jnp.where(mirror, (LANES - lane) % LANES, lane)
    slots = out_ref.shape[0]
    for i, source in enumerate((before, head, tail, after)):
        load_rows(rows_ref, i * REACH, source.at[0, 0])
    powers = {}
    for s in range(-REACH, slots):
        terms = []
        if s < 0 or s >= slots - REACH:
            j = s % REACH
            at = j if s < 0 else 2 * REACH + j
            terms.append(cross_tile(rows_ref, at, range(REACH - j, REACH + 1)))
        if s in OUTER:
            terms.append(outer_ref[0, OUTER.index(s)])
        if 4 <= s < 20:
            terms.append(inner_ref[0, s - 4])
        value = jnp.take_along_axis(sum(terms[1:], terms[0]), order, axis=1)
        powers[s] = jnp.where(valid_ref[s + REACH] > 0.0, value * (1.0 / 64.0), 0.0)
        if s >= 0:
            out_ref[s, pl.ds(0, REACH), :] = powers[s]
            backward = powers[s - 1]
            for k in range(2, REACH + 1):
                backward = jnp.where(row == k - 1, powers[s - k], backward)
            out_ref[s, pl.ds(REACH, REACH), :] = backward


CHUNKS = 4


def cross_call(kernel, name, operands, specs, out_specs, out_shape, held, pairs):
    rows = 128
    return pl.pallas_call(
        kernel,
        grid=(2, CHUNKS),
        in_specs=specs,
        out_specs=out_specs,
        out_shape=out_shape,
        scratch_shapes=[pltpu.VMEM((held, rows, LANES), jnp.float32)],
        compiler_params=pltpu.CompilerParams(vmem_limit_bytes=24 * MIB),
        cost_estimate=pl.CostEstimate(
            flops=2 * pairs * rows * 1024,
            bytes_accessed=2 * held * rows * 1024,
            transcendentals=0,
        ),
        name=name,
    )(*operands)


def spectra_spec(array):
    return pl.BlockSpec((1, 1) + array.shape[2:], lambda i, j: (i, j, 0, 0, 0))


def sums_spec(slots):
    return pl.BlockSpec((1, slots, REACH, LANES), lambda i, j: (i * CHUNKS + j, 0, 0, 0))


def outer_powers(head, middle, tail):
    slots = len(OUTER)
    return cross_call(
        outer_kernel,
        "outer_pairs",
        [in_hbm(head), in_hbm(middle), in_hbm(tail)],
        [spectra_spec(head)] * 3,
        sums_spec(slots),
        pltpu.HBM((2 * CHUNKS, slots, REACH, LANES), jnp.float32),
        slots,
        120,
    )


def inner_powers(head, middle, inner, tail):
    return cross_call(
        inner_kernel,
        "inner_pairs",
        [in_hbm(head), in_hbm(middle), in_hbm(inner), in_hbm(tail)],
        [spectra_spec(head)] * 4,
        sums_spec(2 * REACH),
        pltpu.HBM((2 * CHUNKS, 2 * REACH, REACH, LANES), jnp.float32),
        3 * REACH,
        100,
    )


def final_powers(before, head, tail, after, outer_sums, inner_sums, valid):
    slots = 4 * REACH
    spectra_specs = [spectra_spec(array) for array in (before, head, tail, after)]
    return cross_call(
        final_kernel,
        "pair_power",
        [before, in_hbm(head), in_hbm(tail), after, in_hbm(outer_sums), in_hbm(inner_sums), valid],
        spectra_specs
        + [
            sums_spec(outer_sums.shape[1]),
            sums_spec(inner_sums.shape[1]),
            pl.BlockSpec(valid.shape, lambda i, j: (0, 0, 0)),
        ],
        pl.BlockSpec(
            (slots, 2 * REACH, LANES),
            lambda i, j: (0, 0, jnp.where(i == 0, j, 2 * CHUNKS - 1 - j)),
        ),
        jax.ShapeDtypeStruct((slots, 2 * REACH, 2 * CHUNKS * LANES), jnp.float32),
        slots,
        72,
    )


def body(visibilities, owner_order, group_ids, partner_flags):
    n_tm = lax.axis_size("tm")
    n_chan = lax.axis_size("chan")
    n_dev = n_tm * n_chan
    count, n_base, _, width = visibilities.shape
    per = n_base // n_dev

    table = half_table(width * n_chan)

    start = lax.axis_index(AXES) * per
    groups = lax.dynamic_slice_in_dim(
        jnp.pad(group_ids, (REACH, REACH), constant_values=-1), start, per + 2 * REACH, 0
    )
    flags = lax.dynamic_slice_in_dim(
        jnp.pad(partner_flags, ((REACH, REACH), (0, 0))), start, per + REACH, 0
    )
    own_group = groups[: per + REACH]
    same = jnp.stack([groups[k : k + per + REACH] == own_group for k in range(1, REACH + 1)], 1)
    valid = jnp.broadcast_to(
        (same & (flags == 1)).astype(jnp.float32)[:, :, None], (per + REACH, REACH, LANES)
    )

    def exchange(slots, earlier):
        send = gather(visibilities, owner_order, slots, n_dev, earlier)
        send = send.reshape(n_dev, 2 * count * len(slots), width)
        return lax.all_to_all(send, AXES, 0, 0, tiled=True)

    up = [(i, i + 1) for i in range(n_dev - 1)]
    down = [(i + 1, i) for i in range(n_dev - 1)]
    received_outer = exchange(OUTER, group_ids)
    received_inner = exchange(INNER, table)
    head = spectra(received_outer, table, n_tm, n_chan, 0, REACH, group_ids)
    tail = spectra(received_outer, table, n_tm, n_chan, 2 * REACH, REACH, group_ids)
    after = lax.ppermute(head, AXES, down)
    before = lax.ppermute(tail, AXES, up)
    middle = spectra(received_outer, table, n_tm, n_chan, REACH, REACH, group_ids)
    outer_sums = outer_powers(head, middle, tail)
    inner = spectra(received_inner, table, n_tm, n_chan, 0, REACH, outer_sums)
    inner_sums = inner_powers(head, middle, inner, tail)
    return final_powers(before, head, tail, after, outer_sums, inner_sums, valid)


def solution(mesh):
    return jax.shard_map(
        body,
        mesh=mesh,
        in_specs=(P("tm", None, None, "chan"), P(), P(), P()),
        out_specs=P(AXES, None, None),
        check_vma=False,
    )
```

```python
import functools
import math

import jax
import jax.numpy as jnp
from jax import lax
from jax.experimental import pallas as pl
from jax.experimental.pallas import tpu as pltpu
from jax.sharding import PartitionSpec as P

AXES = ("tm", "chan")
MIB = 2**20
LANES = 128
REACH = 8
OUTER = tuple(range(8)) + tuple(range(24, 32))
INNER = tuple(range(8, 24))


def in_hbm(array):
    return pltpu.with_memory_space_constraint(array, pltpu.HBM)


def half_table(n_chan):
    channel_index = jnp.arange(n_chan, dtype=jnp.int32)
    place = jnp.arange(n_chan, dtype=jnp.int32)
    delay_index = place // (2 * LANES) * LANES + place % LANES
    is_sine = place % (2 * LANES) >= LANES
    middle = is_sine & (delay_index == 0)
    delay_index = jnp.where(middle, n_chan // 2, delay_index)
    turn = jnp.where(is_sine & ~middle, 3 * n_chan // 4, 0)
    phase_index = (channel_index[:, None] * delay_index[None, :] + turn[None, :]) % n_chan
    phase_angle = 2.0 * math.pi / n_chan * phase_index.astype(jnp.float32)
    base_angle = 2.0 * math.pi / n_chan * channel_index.astype(jnp.float32)
    window_taper = (
        0.35875
        - 0.48829 * jnp.cos(base_angle)
        + 0.14128 * jnp.cos(2.0 * base_angle)
        - 0.01168 * jnp.cos(3.0 * base_angle)
    )
    weights_norm = window_taper / jnp.sqrt(jnp.sum(window_taper * window_taper))
    return (weights_norm[:, None] * jnp.cos(phase_angle)).astype(jnp.bfloat16)


def gather_kernel(slots, per, order_ref, vis_ref, _, out_ref):
    owners, count = out_ref.shape[0], out_ref.shape[2]
    first = pl.program_id(0) * owners

    def one_owner(owner, carry):
        base = (first + owner) * per
        for j, slot in enumerate(slots):
            source = order_ref[base + slot]
            for t in range(count):
                out_ref[owner, j, t] = vis_ref[t, source]
        return carry

    lax.fori_loop(0, owners, one_owner, 0)


def gather(visibilities, order, slots, n_dev, earlier):
    count, n_base = visibilities.shape[:2]
    tail = visibilities.shape[2:]
    steps = 8
    return pl.pallas_call(
        functools.partial(gather_kernel, slots, n_base // n_dev),
        grid_spec=pltpu.PrefetchScalarGridSpec(
            num_scalar_prefetch=1,
            grid=(steps,),
            in_specs=[
                pl.BlockSpec(memory_space=pltpu.VMEM),
                pl.BlockSpec(memory_space=pl.ANY),
            ],
            out_specs=pl.BlockSpec(
                (n_dev // steps, len(slots), count) + tail, lambda i, o: (i, 0, 0, 0, 0)
            ),
        ),
        out_shape=pltpu.HBM((n_dev, len(slots), count) + tail, visibilities.dtype),
        compiler_params=pltpu.CompilerParams(vmem_limit_bytes=24 * MIB),
        cost_estimate=pl.CostEstimate(
            flops=0, bytes_accessed=2 * count * n_dev * len(slots) * 512, transcendentals=0
        ),
        name="slot_gather",
    )(in_hbm(order), visibilities, in_hbm(earlier))


def spectra_kernel(received_ref, table_ref, _, out_ref):
    sources, n_chan, rows = received_ref.shape[:3]
    slots = out_ref.shape[2]
    n_rows = sources * rows
    block = jnp.concatenate(
        [received_ref[:, c].reshape(n_rows, LANES) for c in range(n_chan)], axis=1
    )
    chunks = table_ref.shape[1] // (2 * LANES)
    shape = (n_rows // 8, 8, LANES)
    first = lax.broadcasted_iota(jnp.int32, shape, 2) == 0
    is_real = lax.broadcasted_iota(jnp.int32, shape, 1) % 2 == 0

    def store(sign, c, value):
        value = jnp.swapaxes(value.reshape(sources, slots, 8, LANES), 0, 1)
        value = value.reshape(slots, sources * 8, LANES).astype(jnp.bfloat16)
        out_ref[sign, c] = value

    minus = []
    for c in range(chunks):
        both = jnp.dot(
            block, table_ref[:, pl.ds(2 * c * LANES, 2 * LANES)], preferred_element_type=jnp.float32
        )
        cosine, sine = both[:, :LANES].reshape(shape), both[:, LANES:].reshape(shape)
        other = jnp.where(is_real, pltpu.roll(sine, 7, 1), -pltpu.roll(sine, 1, 1))
        ahead, back = cosine + other, cosine - other
        if c == 0:
            ahead, back = jnp.where(first, cosine, ahead), jnp.where(first, sine, back)
        store(0, c, ahead)
        minus.append(back)
        if c > 0:
            store(1, c - 1, jnp.where(first, back, minus[c - 1]))
    store(1, chunks - 1, jnp.where(first, minus[0], minus[-1]))


def spectra(received, table, n_tm, n_chan, first, slots, earlier):
    _, pairs, lanes = received.shape
    step = REACH
    width = table.shape[1]
    rows = n_tm * 8
    chunks = width // (2 * LANES)
    return pl.pallas_call(
        spectra_kernel,
        grid=(slots // step,),
        in_specs=[
            pl.BlockSpec(
                (n_tm, n_chan, 8 * step, lanes), lambda t: (0, 0, first // step + t, 0)
            ),
            pl.BlockSpec(table.shape, lambda t: (0, 0), pipeline_mode=pl.Buffered(1)),
            pl.BlockSpec(memory_space=pl.ANY),
        ],
        out_specs=pl.BlockSpec((2, chunks, step, rows, LANES), lambda t: (0, 0, t, 0, 0)),
        out_shape=pltpu.HBM((2, chunks, slots, rows, LANES), jnp.bfloat16),
        compiler_params=pltpu.CompilerParams(vmem_limit_bytes=32 * MIB),
        cost_estimate=pl.CostEstimate(
            flops=16 * slots * n_tm * width * width,
            bytes_accessed=64 * slots * n_tm * width,
            transcendentals=0,
        ),
        name="delay_spectra",
    )(in_hbm(received.reshape(n_tm, n_chan, pairs, lanes)), in_hbm(table), in_hbm(earlier))


def fold_rows(sums):
    row = lax.broadcasted_iota(jnp.int32, sums[0].shape, 0)
    for bit in (1, 2, 4):
        low = (row & bit) == 0
        merged = []
        for i in range(0, len(sums), 2):
            a, b = sums[i], sums[i + 1]
            kept, moved = jnp.where(low, a, b), jnp.where(low, b, a)
            merged.append(kept + pltpu.roll(moved, 8 - bit, 0))
        sums = merged
    return sums[0]


def cross_tile(rows_ref, s, offsets):
    spans = [pl.ds(8 * g, 8) for g in range(rows_ref.shape[1] // 8)]
    own = [rows_ref[s, span] for span in spans]
    sums = []
    for k in range(1, REACH + 1):
        if k not in offsets:
            sums.append(jnp.zeros((8, LANES), jnp.float32))
            continue
        total = None
        for g, span in enumerate(spans):
            term = own[g] * rows_ref[s + k, span]
            total = term if total is None else total + term
        sums.append(total)
    return fold_rows(sums)


def load_rows(target, at, source):
    target[pl.ds(at, source.shape[0])] = source[...].astype(jnp.float32)


def outer_kernel(head, tail, out_ref, rows_ref):
    def one_chunk(c, carry):
        load_rows(rows_ref, 0, head.at[0, c])
        load_rows(rows_ref, REACH, tail.at[0, c])
        for first in (0, REACH):
            for j in range(REACH):
                out_ref[c, first + j] = cross_tile(rows_ref, first + j, range(1, REACH - j))
        return carry

    lax.fori_loop(0, STEP, one_chunk, 0)


def inner_kernel(head, inner, tail, out_ref, rows_ref):
    def one_chunk(c, carry):
        load_rows(rows_ref, 0, head.at[0, c])
        load_rows(rows_ref, REACH, inner.at[0, c])
        load_rows(rows_ref, 3 * REACH, tail.at[0, c])
        for s in range(3 * REACH):
            out_ref[c, s] = cross_tile(rows_ref, s, range(max(1, REACH - s), REACH + 1))
        return carry

    lax.fori_loop(0, STEP, one_chunk, 0)


def final_kernel(before, head, tail, after, outer_ref, inner_ref, valid_ref, out_ref, rows_ref):
    shape = (REACH, LANES)
    lane = lax.broadcasted_iota(jnp.int32, shape, 1)
    row = lax.broadcasted_iota(jnp.int32, shape, 0)
    mirror = pl.program_id(0) == 1
    order = jnp.where(mirror, (LANES - lane) % LANES, lane)
    slots = out_ref.shape[0]

    def one_chunk(c, carry):
        at = jnp.where(mirror, STEP - 1 - c, c)
        lanes = pl.ds(pl.multiple_of(at * LANES, LANES), LANES)
        for i, source in enumerate((before, head, tail, after)):
            load_rows(rows_ref, i * REACH, source.at[0, c])
        powers = {}
        for s in range(-REACH, slots):
            terms = []
            if s < 0 or s >= slots - REACH:
                j = s % REACH
                start = j if s < 0 else 2 * REACH + j
                terms.append(cross_tile(rows_ref, start, range(REACH - j, REACH + 1)))
            if s in OUTER:
                terms.append(outer_ref[c, OUTER.index(s)])
            if 0 <= s < slots - REACH:
                terms.append(inner_ref[c, s])
            value = jnp.take_along_axis(sum(terms[1:], terms[0]), order, axis=1)
            powers[s] = jnp.where(valid_ref[s + REACH] > 0.0, value * (1.0 / 64.0), 0.0)
            if s >= 0:
                out_ref[s, pl.ds(0, REACH), lanes] = powers[s]
                backward = powers[s - 1]
                for k in range(2, REACH + 1):
                    backward = jnp.where(row == k - 1, powers[s - k], backward)
                out_ref[s, pl.ds(REACH, REACH), lanes] = backward
        return carry

    lax.fori_loop(0, STEP, one_chunk, 0)


CHUNKS, STEP = 4, 2


def cross_call(kernel, name, operands, specs, out_specs, out_shape, held, pairs):
    rows = 128
    return pl.pallas_call(
        kernel,
        grid=(2, CHUNKS // STEP),
        in_specs=specs,
        out_specs=out_specs,
        out_shape=out_shape,
        scratch_shapes=[pltpu.VMEM((held, rows, LANES), jnp.float32)],
        compiler_params=pltpu.CompilerParams(vmem_limit_bytes=32 * MIB),
        cost_estimate=pl.CostEstimate(
            flops=2 * pairs * rows * 1024,
            bytes_accessed=2 * held * rows * 1024,
            transcendentals=0,
        ),
        name=name,
    )(*operands)


def spectra_spec(array):
    return pl.BlockSpec((1, STEP) + array.shape[2:], lambda i, j: (i, j, 0, 0, 0))


def sums_spec(slots):
    return pl.BlockSpec(
        (STEP, slots, REACH, LANES), lambda i, j: (i * (CHUNKS // STEP) + j, 0, 0, 0)
    )


def outer_powers(head, tail):
    slots = 2 * REACH
    return cross_call(
        outer_kernel,
        "outer_pairs",
        [in_hbm(head), in_hbm(tail)],
        [spectra_spec(head)] * 2,
        sums_spec(slots),
        pltpu.HBM((2 * CHUNKS, slots, REACH, LANES), jnp.float32),
        slots,
        56,
    )


def inner_powers(head, inner, tail):
    slots = 3 * REACH
    return cross_call(
        inner_kernel,
        "inner_pairs",
        [in_hbm(head), in_hbm(inner), in_hbm(tail)],
        [spectra_spec(array) for array in (head, inner, tail)],
        sums_spec(slots),
        pltpu.HBM((2 * CHUNKS, slots, REACH, LANES), jnp.float32),
        4 * REACH,
        164,
    )


def final_powers(before, head, tail, after, outer_sums, inner_sums, valid):
    slots = 4 * REACH
    spectra_specs = [spectra_spec(array) for array in (before, head, tail, after)]
    return cross_call(
        final_kernel,
        "pair_power",
        [before, in_hbm(head), in_hbm(tail), after, in_hbm(outer_sums), in_hbm(inner_sums), valid],
        spectra_specs
        + [
            sums_spec(outer_sums.shape[1]),
            sums_spec(inner_sums.shape[1]),
            pl.BlockSpec(valid.shape, lambda i, j: (0, 0, 0)),
        ],
        pl.BlockSpec(
            (slots, 2 * REACH, STEP * LANES),
            lambda i, j: (0, 0, jnp.where(i == 0, j, 2 * CHUNKS // STEP - 1 - j)),
        ),
        jax.ShapeDtypeStruct((slots, 2 * REACH, 2 * CHUNKS * LANES), jnp.float32),
        slots,
        72,
    )


def body(visibilities, owner_order, group_ids, partner_flags):
    n_tm = lax.axis_size("tm")
    n_chan = lax.axis_size("chan")
    n_dev = n_tm * n_chan
    count, n_base, _, width = visibilities.shape
    per = n_base // n_dev

    table = half_table(width * n_chan)

    start = lax.axis_index(AXES) * per
    groups = lax.dynamic_slice_in_dim(
        jnp.pad(group_ids, (REACH, REACH), constant_values=-1), start, per + 2 * REACH, 0
    )
    flags = lax.dynamic_slice_in_dim(
        jnp.pad(partner_flags, ((REACH, REACH), (0, 0))), start, per + REACH, 0
    )
    own_group = groups[: per + REACH]
    same = jnp.stack([groups[k : k + per + REACH] == own_group for k in range(1, REACH + 1)], 1)
    valid = jnp.broadcast_to(
        (same & (flags == 1)).astype(jnp.float32)[:, :, None], (per + REACH, REACH, LANES)
    )

    def exchange(slots, earlier):
        send = gather(visibilities, owner_order, slots, n_dev, earlier)
        send = send.reshape(n_dev, 2 * count * len(slots), width)
        return lax.all_to_all(send, AXES, 0, 0, tiled=True)

    up = [(i, i + 1) for i in range(n_dev - 1)]
    down = [(i + 1, i) for i in range(n_dev - 1)]
    received_outer = exchange(OUTER, group_ids)
    received_inner = exchange(INNER, group_ids)
    head = spectra(received_outer, table, n_tm, n_chan, 0, REACH, group_ids)
    tail = spectra(received_outer, table, n_tm, n_chan, REACH, REACH, group_ids)
    after = lax.ppermute(head, AXES, down)
    before = lax.ppermute(tail, AXES, up)
    outer_sums = outer_powers(head, tail)
    inner = spectra(received_inner, table, n_tm, n_chan, 0, 2 * REACH, outer_sums)
    inner_sums = inner_powers(head, inner, tail)
    return final_powers(before, head, tail, after, outer_sums, inner_sums, valid)


def solution(mesh):
    return jax.shard_map(
        body,
        mesh=mesh,
        in_specs=(P("tm", None, None, "chan"), P(), P(), P()),
        out_specs=P(AXES, None, None),
        check_vma=False,
    )
```

```python
import functools
import math

import jax
import jax.numpy as jnp
from jax import lax
from jax.experimental import pallas as pl
from jax.experimental.pallas import tpu as pltpu
from jax.sharding import PartitionSpec as P

AXES = ("tm", "chan")
MIB = 2**20
LANES = 128
REACH = 8
OUTER = tuple(range(8)) + tuple(range(24, 32))
INNER = tuple(range(8, 24))


def in_hbm(array):
    return pltpu.with_memory_space_constraint(array, pltpu.HBM)


def half_table(n_chan):
    channel_index = jnp.arange(n_chan, dtype=jnp.int32)
    place = jnp.arange(n_chan, dtype=jnp.int32)
    delay_index = place // (2 * LANES) * LANES + place % LANES
    is_sine = place % (2 * LANES) >= LANES
    middle = is_sine & (delay_index == 0)
    delay_index = jnp.where(middle, n_chan // 2, delay_index)
    turn = jnp.where(is_sine & ~middle, 3 * n_chan // 4, 0)
    phase_index = (channel_index[:, None] * delay_index[None, :] + turn[None, :]) % n_chan
    phase_angle = 2.0 * math.pi / n_chan * phase_index.astype(jnp.float32)
    base_angle = 2.0 * math.pi / n_chan * channel_index.astype(jnp.float32)
    window_taper = (
        0.35875
        - 0.48829 * jnp.cos(base_angle)
        + 0.14128 * jnp.cos(2.0 * base_angle)
        - 0.01168 * jnp.cos(3.0 * base_angle)
    )
    weights_norm = window_taper / jnp.sqrt(jnp.sum(window_taper * window_taper))
    return (weights_norm[:, None] * jnp.cos(phase_angle)).astype(jnp.bfloat16)


def gather_kernel(slots, per, order_ref, vis_ref, _, out_ref, vis, rows, load_sems, store_sems):
    count = vis.shape[0]
    half = count // 2
    loads = [
        pltpu.make_async_copy(
            vis_ref.at[pl.ds(h * half, half)], vis.at[pl.ds(h * half, half)], load_sems.at[h]
        )
        for h in range(2)
    ]
    for load in loads:
        load.start()
    n_dev = out_ref.shape[0]
    groups = store_sems.shape[0]
    owners = n_dev // groups

    def sort_half(h, first, number):
        def one_owner(i, carry):
            owner = first + i
            base = owner * per
            for j, slot in enumerate(slots):
                source = order_ref[base + slot]
                for t in range(h * half, (h + 1) * half):
                    rows[owner, j, t] = vis[t, source]
            return carry

        lax.fori_loop(0, number, one_owner, 0)

    loads[0].wait()
    sort_half(0, 0, n_dev)
    loads[1].wait()
    stores = []
    for g in range(groups):
        sort_half(1, g * owners, owners)
        span = pl.ds(g * owners, owners)
        store = pltpu.make_async_copy(rows.at[span], out_ref.at[span], store_sems.at[g])
        store.start()
        stores.append(store)
    for store in stores:
        store.wait()


def gather(visibilities, order, slots, n_dev, earlier):
    count, n_base = visibilities.shape[:2]
    tail = visibilities.shape[2:]
    groups = 8
    shape = (n_dev, len(slots), count) + tail
    anywhere = pl.BlockSpec(memory_space=pl.ANY)
    return pl.pallas_call(
        functools.partial(gather_kernel, slots, n_base // n_dev),
        grid_spec=pltpu.PrefetchScalarGridSpec(
            num_scalar_prefetch=1,
            grid=(),
            in_specs=[anywhere] * 2,
            out_specs=anywhere,
            scratch_shapes=[
                pltpu.VMEM(visibilities.shape, visibilities.dtype),
                pltpu.VMEM(shape, visibilities.dtype),
                pltpu.SemaphoreType.DMA((2,)),
                pltpu.SemaphoreType.DMA((groups,)),
            ],
        ),
        out_shape=pltpu.HBM(shape, visibilities.dtype),
        compiler_params=pltpu.CompilerParams(vmem_limit_bytes=24 * MIB),
        cost_estimate=pl.CostEstimate(
            flops=0, bytes_accessed=2 * count * n_dev * len(slots) * 512, transcendentals=0
        ),
        name="slot_gather",
    )(in_hbm(order), in_hbm(visibilities), in_hbm(earlier))


def spectra_kernel(received_ref, table_ref, _, out_ref):
    sources, n_chan, rows = received_ref.shape[:3]
    slots = out_ref.shape[2]
    n_rows = sources * rows
    block = jnp.concatenate(
        [received_ref[:, c].reshape(n_rows, LANES) for c in range(n_chan)], axis=1
    )
    chunks = table_ref.shape[1] // (2 * LANES)
    shape = (n_rows // 8, 8, LANES)
    first = lax.broadcasted_iota(jnp.int32, shape, 2) == 0
    is_real = lax.broadcasted_iota(jnp.int32, shape, 1) % 2 == 0

    def store(sign, c, value):
        value = jnp.swapaxes(value.reshape(sources, slots, 8, LANES), 0, 1)
        value = value.reshape(slots, sources * 8, LANES).astype(jnp.bfloat16)
        out_ref[sign, c] = value

    minus = []
    for c in range(chunks):
        both = jnp.dot(
            block, table_ref[:, pl.ds(2 * c * LANES, 2 * LANES)], preferred_element_type=jnp.float32
        )
        cosine, sine = both[:, :LANES].reshape(shape), both[:, LANES:].reshape(shape)
        other = jnp.where(is_real, pltpu.roll(sine, 7, 1), -pltpu.roll(sine, 1, 1))
        ahead, back = cosine + other, cosine - other
        if c == 0:
            ahead, back = jnp.where(first, cosine, ahead), jnp.where(first, sine, back)
        store(0, c, ahead)
        minus.append(back)
        if c > 0:
            store(1, c - 1, jnp.where(first, back, minus[c - 1]))
    store(1, chunks - 1, jnp.where(first, minus[0], minus[-1]))


def spectra(received, table, n_tm, n_chan, first, slots, earlier):
    _, pairs, lanes = received.shape
    step = REACH
    width = table.shape[1]
    rows = n_tm * 8
    chunks = width // (2 * LANES)
    return pl.pallas_call(
        spectra_kernel,
        grid=(slots // step,),
        in_specs=[
            pl.BlockSpec(
                (n_tm, n_chan, 8 * step, lanes), lambda t: (0, 0, first // step + t, 0)
            ),
            pl.BlockSpec(table.shape, lambda t: (0, 0), pipeline_mode=pl.Buffered(1)),
            pl.BlockSpec(memory_space=pl.ANY),
        ],
        out_specs=pl.BlockSpec((2, chunks, step, rows, LANES), lambda t: (0, 0, t, 0, 0)),
        out_shape=pltpu.HBM((2, chunks, slots, rows, LANES), jnp.bfloat16),
        compiler_params=pltpu.CompilerParams(vmem_limit_bytes=32 * MIB),
        cost_estimate=pl.CostEstimate(
            flops=16 * slots * n_tm * width * width,
            bytes_accessed=64 * slots * n_tm * width,
            transcendentals=0,
        ),
        name="delay_spectra",
    )(in_hbm(received.reshape(n_tm, n_chan, pairs, lanes)), in_hbm(table), in_hbm(earlier))


def fold_rows(sums):
    row = lax.broadcasted_iota(jnp.int32, sums[0].shape, 0)
    for bit in (1, 2, 4):
        low = (row & bit) == 0
        merged = []
        for i in range(0, len(sums), 2):
            a, b = sums[i], sums[i + 1]
            kept, moved = jnp.where(low, a, b), jnp.where(low, b, a)
            merged.append(kept + pltpu.roll(moved, 8 - bit, 0))
        sums = merged
    return sums[0]


def cross_tile(rows_ref, s, offsets):
    spans = [pl.ds(8 * g, 8) for g in range(rows_ref.shape[1] // 8)]
    own = [rows_ref[s, span] for span in spans]
    sums = []
    for k in range(1, REACH + 1):
        if k not in offsets:
            sums.append(jnp.zeros((8, LANES), jnp.float32))
            continue
        total = None
        for g, span in enumerate(spans):
            term = own[g] * rows_ref[s + k, span]
            total = term if total is None else total + term
        sums.append(total)
    return fold_rows(sums)


def load_rows(target, at, source):
    target[pl.ds(at, source.shape[0])] = source[...].astype(jnp.float32)


def outer_kernel(head, tail, out_ref, rows_ref):
    def one_chunk(c, carry):
        load_rows(rows_ref, 0, head.at[0, c])
        load_rows(rows_ref, REACH, tail.at[0, c])
        for first in (0, REACH):
            for j in range(REACH):
                out_ref[c, first + j] = cross_tile(rows_ref, first + j, range(1, REACH - j))
        return carry

    lax.fori_loop(0, STEP, one_chunk, 0)


def inner_kernel(head, inner, tail, out_ref, rows_ref):
    def one_chunk(c, carry):
        load_rows(rows_ref, 0, head.at[0, c])
        load_rows(rows_ref, REACH, inner.at[0, c])
        load_rows(rows_ref, 3 * REACH, tail.at[0, c])
        for s in range(3 * REACH):
            out_ref[c, s] = cross_tile(rows_ref, s, range(max(1, REACH - s), REACH + 1))
        return carry

    lax.fori_loop(0, STEP, one_chunk, 0)


def final_kernel(before, head, tail, after, outer_ref, inner_ref, valid_ref, out_ref, rows_ref):
    shape = (REACH, LANES)
    lane = lax.broadcasted_iota(jnp.int32, shape, 1)
    row = lax.broadcasted_iota(jnp.int32, shape, 0)
    mirror = pl.program_id(0) == 1
    order = jnp.where(mirror, (LANES - lane) % LANES, lane)
    slots = out_ref.shape[0]

    def one_chunk(c, carry):
        at = jnp.where(mirror, STEP - 1 - c, c)
        lanes = pl.ds(pl.multiple_of(at * LANES, LANES), LANES)
        for i, source in enumerate((before, head, tail, after)):
            load_rows(rows_ref, i * REACH, source.at[0, c])
        powers = {}
        for s in range(-REACH, slots):
            terms = []
            if s < 0 or s >= slots - REACH:
                j = s % REACH
                start = j if s < 0 else 2 * REACH + j
                terms.append(cross_tile(rows_ref, start, range(REACH - j, REACH + 1)))
            if s in OUTER:
                terms.append(outer_ref[c, OUTER.index(s)])
            if 0 <= s < slots - REACH:
                terms.append(inner_ref[c, s])
            value = jnp.take_along_axis(sum(terms[1:], terms[0]), order, axis=1)
            powers[s] = jnp.where(valid_ref[s + REACH] > 0.0, value * (1.0 / 64.0), 0.0)
            if s >= 0:
                out_ref[s, pl.ds(0, REACH), lanes] = powers[s]
                backward = powers[s - 1]
                for k in range(2, REACH + 1):
                    backward = jnp.where(row == k - 1, powers[s - k], backward)
                out_ref[s, pl.ds(REACH, REACH), lanes] = backward
        return carry

    lax.fori_loop(0, STEP, one_chunk, 0)


CHUNKS, STEP = 4, 2


def cross_call(kernel, name, operands, specs, out_specs, out_shape, held, pairs):
    rows = 128
    return pl.pallas_call(
        kernel,
        grid=(2, CHUNKS // STEP),
        in_specs=specs,
        out_specs=out_specs,
        out_shape=out_shape,
        scratch_shapes=[pltpu.VMEM((held, rows, LANES), jnp.float32)],
        compiler_params=pltpu.CompilerParams(vmem_limit_bytes=32 * MIB),
        cost_estimate=pl.CostEstimate(
            flops=2 * pairs * rows * 1024,
            bytes_accessed=2 * held * rows * 1024,
            transcendentals=0,
        ),
        name=name,
    )(*operands)


def spectra_spec(array):
    return pl.BlockSpec((1, STEP) + array.shape[2:], lambda i, j: (i, j, 0, 0, 0))


def sums_spec(slots):
    return pl.BlockSpec(
        (STEP, slots, REACH, LANES), lambda i, j: (i * (CHUNKS // STEP) + j, 0, 0, 0)
    )


def outer_powers(head, tail):
    slots = 2 * REACH
    return cross_call(
        outer_kernel,
        "outer_pairs",
        [in_hbm(head), in_hbm(tail)],
        [spectra_spec(head)] * 2,
        sums_spec(slots),
        pltpu.HBM((2 * CHUNKS, slots, REACH, LANES), jnp.float32),
        slots,
        56,
    )


def inner_powers(head, inner, tail):
    slots = 3 * REACH
    return cross_call(
        inner_kernel,
        "inner_pairs",
        [in_hbm(head), in_hbm(inner), in_hbm(tail)],
        [spectra_spec(array) for array in (head, inner, tail)],
        sums_spec(slots),
        pltpu.HBM((2 * CHUNKS, slots, REACH, LANES), jnp.float32),
        4 * REACH,
        164,
    )


def final_powers(before, head, tail, after, outer_sums, inner_sums, valid):
    slots = 4 * REACH
    spectra_specs = [spectra_spec(array) for array in (before, head, tail, after)]
    return cross_call(
        final_kernel,
        "pair_power",
        [before, in_hbm(head), in_hbm(tail), after, in_hbm(outer_sums), in_hbm(inner_sums), valid],
        spectra_specs
        + [
            sums_spec(outer_sums.shape[1]),
            sums_spec(inner_sums.shape[1]),
            pl.BlockSpec(valid.shape, lambda i, j: (0, 0, 0)),
        ],
        pl.BlockSpec(
            (slots, 2 * REACH, STEP * LANES),
            lambda i, j: (0, 0, jnp.where(i == 0, j, 2 * CHUNKS // STEP - 1 - j)),
        ),
        jax.ShapeDtypeStruct((slots, 2 * REACH, 2 * CHUNKS * LANES), jnp.float32),
        slots,
        72,
    )


def after_those(arrays, *earlier):
    def kernel(*refs):
        pass

    count = len(arrays)
    anywhere = pl.BlockSpec(memory_space=pl.ANY)
    return pl.pallas_call(
        kernel,
        in_specs=[anywhere] * (count + len(earlier)),
        out_specs=[anywhere] * count,
        out_shape=[pltpu.HBM(array.shape, array.dtype) for array in arrays],
        input_output_aliases={i: i for i in range(count)},
        name="in_order",
    )(*[in_hbm(array) for array in arrays], *earlier)


def body(visibilities, owner_order, group_ids, partner_flags):
    n_tm = lax.axis_size("tm")
    n_chan = lax.axis_size("chan")
    n_dev = n_tm * n_chan
    count, n_base, _, width = visibilities.shape
    per = n_base // n_dev

    table = half_table(width * n_chan)

    start = lax.axis_index(AXES) * per
    groups = lax.dynamic_slice_in_dim(
        jnp.pad(group_ids, (REACH, REACH), constant_values=-1), start, per + 2 * REACH, 0
    )
    flags = lax.dynamic_slice_in_dim(
        jnp.pad(partner_flags, ((REACH, REACH), (0, 0))), start, per + REACH, 0
    )
    own_group = groups[: per + REACH]
    same = jnp.stack([groups[k : k + per + REACH] == own_group for k in range(1, REACH + 1)], 1)
    valid = jnp.broadcast_to(
        (same & (flags == 1)).astype(jnp.float32)[:, :, None], (per + REACH, REACH, LANES)
    )

    def exchange(slots, earlier):
        send = gather(visibilities, owner_order, slots, n_dev, earlier)
        send = send.reshape(n_dev, 2 * count * len(slots), width)
        return lax.all_to_all(send, AXES, 0, 0, tiled=True)

    up = [(i, i + 1) for i in range(n_dev - 1)]
    down = [(i + 1, i) for i in range(n_dev - 1)]
    received_outer = exchange(OUTER, group_ids)
    received_inner = exchange(INNER, group_ids)
    head = spectra(received_outer, table, n_tm, n_chan, 0, REACH, group_ids)
    tail = spectra(received_outer, table, n_tm, n_chan, REACH, REACH, group_ids)
    outer_sums = outer_powers(head, tail)
    head_sent, tail_sent = after_those((head, tail), in_hbm(outer_sums))
    after = lax.ppermute(head_sent, AXES, down)
    before = lax.ppermute(tail_sent, AXES, up)
    inner = spectra(received_inner, table, n_tm, n_chan, 0, 2 * REACH, outer_sums)
    inner_sums = inner_powers(head_sent, inner, tail_sent)
    return final_powers(before, head_sent, tail_sent, after, outer_sums, inner_sums, valid)


def solution(mesh):
    return jax.shard_map(
        body,
        mesh=mesh,
        in_specs=(P("tm", None, None, "chan"), P(), P(), P()),
        out_specs=P(AXES, None, None),
        check_vma=False,
    )
```

```python
import functools
import math

import jax
import jax.numpy as jnp
from jax import lax
from jax.experimental import pallas as pl
from jax.experimental.pallas import tpu as pltpu
from jax.sharding import PartitionSpec as P

AXES = ("tm", "chan")
MIB = 2**20
LANES = 128
REACH = 8
OUTER = tuple(range(8)) + tuple(range(24, 32))
INNER = tuple(range(8, 24))


def in_hbm(array):
    return pltpu.with_memory_space_constraint(array, pltpu.HBM)


def half_table(n_chan):
    channel_index = jnp.arange(n_chan, dtype=jnp.int32)
    place = jnp.arange(n_chan, dtype=jnp.int32)
    delay_index = place // (2 * LANES) * LANES + place % LANES
    is_sine = place % (2 * LANES) >= LANES
    middle = is_sine & (delay_index == 0)
    delay_index = jnp.where(middle, n_chan // 2, delay_index)
    turn = jnp.where(is_sine & ~middle, 3 * n_chan // 4, 0)
    phase_index = (channel_index[:, None] * delay_index[None, :] + turn[None, :]) % n_chan
    phase_angle = 2.0 * math.pi / n_chan * phase_index.astype(jnp.float32)
    base_angle = 2.0 * math.pi / n_chan * channel_index.astype(jnp.float32)
    window_taper = (
        0.35875
        - 0.48829 * jnp.cos(base_angle)
        + 0.14128 * jnp.cos(2.0 * base_angle)
        - 0.01168 * jnp.cos(3.0 * base_angle)
    )
    weights_norm = window_taper / jnp.sqrt(jnp.sum(window_taper * window_taper))
    return (weights_norm[:, None] * jnp.cos(phase_angle)).astype(jnp.bfloat16)


def gather_kernel(slots, per, order_ref, vis_ref, _, out_ref, vis, rows, load_sems, store_sems):
    count = vis.shape[0]
    half = count // 2
    loads = [
        pltpu.make_async_copy(
            vis_ref.at[pl.ds(h * half, half)], vis.at[pl.ds(h * half, half)], load_sems.at[h]
        )
        for h in range(2)
    ]
    for load in loads:
        load.start()
    n_dev = out_ref.shape[0]
    groups = store_sems.shape[0]
    owners = n_dev // groups

    def sort_half(h, first, number):
        def one_owner(i, carry):
            owner = first + i
            base = owner * per
            for j, slot in enumerate(slots):
                source = order_ref[base + slot]
                for t in range(h * half, (h + 1) * half):
                    rows[owner, j, t] = vis[t, source]
            return carry

        lax.fori_loop(0, number, one_owner, 0)

    loads[0].wait()
    sort_half(0, 0, n_dev)
    loads[1].wait()
    stores = []
    for g in range(groups):
        sort_half(1, g * owners, owners)
        span = pl.ds(g * owners, owners)
        store = pltpu.make_async_copy(rows.at[span], out_ref.at[span], store_sems.at[g])
        store.start()
        stores.append(store)
    for store in stores:
        store.wait()


def gather(visibilities, order, slots, n_dev, earlier):
    count, n_base = visibilities.shape[:2]
    tail = visibilities.shape[2:]
    groups = 8
    shape = (n_dev, len(slots), count) + tail
    anywhere = pl.BlockSpec(memory_space=pl.ANY)
    return pl.pallas_call(
        functools.partial(gather_kernel, slots, n_base // n_dev),
        grid_spec=pltpu.PrefetchScalarGridSpec(
            num_scalar_prefetch=1,
            grid=(),
            in_specs=[anywhere] * 2,
            out_specs=anywhere,
            scratch_shapes=[
                pltpu.VMEM(visibilities.shape, visibilities.dtype),
                pltpu.VMEM(shape, visibilities.dtype),
                pltpu.SemaphoreType.DMA((2,)),
                pltpu.SemaphoreType.DMA((groups,)),
            ],
        ),
        out_shape=pltpu.HBM(shape, visibilities.dtype),
        compiler_params=pltpu.CompilerParams(vmem_limit_bytes=24 * MIB),
        cost_estimate=pl.CostEstimate(
            flops=0, bytes_accessed=2 * count * n_dev * len(slots) * 512, transcendentals=0
        ),
        name="slot_gather",
    )(in_hbm(order), in_hbm(visibilities), in_hbm(earlier))


def spectra_kernel(received_ref, table_ref, _, out_ref):
    sources, n_chan, rows = received_ref.shape[:3]
    slots = out_ref.shape[2]
    n_rows = sources * rows
    block = jnp.concatenate(
        [received_ref[:, c].reshape(n_rows, LANES) for c in range(n_chan)], axis=1
    )
    chunks = table_ref.shape[1] // (2 * LANES)
    shape = (n_rows // 8, 8, LANES)
    first = lax.broadcasted_iota(jnp.int32, shape, 2) == 0
    is_real = lax.broadcasted_iota(jnp.int32, shape, 1) % 2 == 0

    def store(sign, c, value):
        value = jnp.swapaxes(value.reshape(sources, slots, 8, LANES), 0, 1)
        value = value.reshape(slots, sources * 8, LANES).astype(jnp.bfloat16)
        out_ref[sign, c] = value

    minus = []
    for c in range(chunks):
        both = jnp.dot(
            block, table_ref[:, pl.ds(2 * c * LANES, 2 * LANES)], preferred_element_type=jnp.float32
        )
        cosine, sine = both[:, :LANES].reshape(shape), both[:, LANES:].reshape(shape)
        other = jnp.where(is_real, pltpu.roll(sine, 7, 1), -pltpu.roll(sine, 1, 1))
        ahead, back = cosine + other, cosine - other
        if c == 0:
            ahead, back = jnp.where(first, cosine, ahead), jnp.where(first, sine, back)
        store(0, c, ahead)
        minus.append(back)
        if c > 0:
            store(1, c - 1, jnp.where(first, back, minus[c - 1]))
    store(1, chunks - 1, jnp.where(first, minus[0], minus[-1]))


def spectra(received, table, n_tm, n_chan, first, slots, earlier):
    _, pairs, lanes = received.shape
    step = REACH
    width = table.shape[1]
    rows = n_tm * 8
    chunks = width // (2 * LANES)
    return pl.pallas_call(
        spectra_kernel,
        grid=(slots // step,),
        in_specs=[
            pl.BlockSpec(
                (n_tm, n_chan, 8 * step, lanes), lambda t: (0, 0, first // step + t, 0)
            ),
            pl.BlockSpec(memory_space=pltpu.VMEM),
            pl.BlockSpec(memory_space=pl.ANY),
        ],
        out_specs=pl.BlockSpec((2, chunks, step, rows, LANES), lambda t: (0, 0, t, 0, 0)),
        out_shape=jax.ShapeDtypeStruct((2, chunks, slots, rows, LANES), jnp.bfloat16),
        compiler_params=pltpu.CompilerParams(vmem_limit_bytes=32 * MIB),
        cost_estimate=pl.CostEstimate(
            flops=16 * slots * n_tm * width * width,
            bytes_accessed=64 * slots * n_tm * width,
            transcendentals=0,
        ),
        name="delay_spectra",
    )(in_hbm(received.reshape(n_tm, n_chan, pairs, lanes)), table, earlier)


def fold_rows(sums):
    row = lax.broadcasted_iota(jnp.int32, sums[0].shape, 0)
    for bit in (1, 2, 4):
        low = (row & bit) == 0
        merged = []
        for i in range(0, len(sums), 2):
            a, b = sums[i], sums[i + 1]
            kept, moved = jnp.where(low, a, b), jnp.where(low, b, a)
            merged.append(kept + pltpu.roll(moved, 8 - bit, 0))
        sums = merged
    return sums[0]


def cross_tile(rows_ref, s, offsets):
    spans = [pl.ds(8 * g, 8) for g in range(rows_ref.shape[1] // 8)]
    own = [rows_ref[s, span] for span in spans]
    sums = []
    for k in range(1, REACH + 1):
        if k not in offsets:
            sums.append(jnp.zeros((8, LANES), jnp.float32))
            continue
        total = None
        for g, span in enumerate(spans):
            term = own[g] * rows_ref[s + k, span]
            total = term if total is None else total + term
        sums.append(total)
    return fold_rows(sums)


def load_rows(target, at, source):
    target[pl.ds(at, source.shape[0])] = source[...].astype(jnp.float32)


def outer_kernel(head, tail, out_ref, rows_ref):
    sign, first_chunk = pl.program_id(0), pl.program_id(1) * STEP

    def one_chunk(c, carry):
        load_rows(rows_ref, 0, head.at[sign, first_chunk + c])
        load_rows(rows_ref, REACH, tail.at[sign, first_chunk + c])
        for first in (0, REACH):
            for j in range(REACH):
                out_ref[c, first + j] = cross_tile(rows_ref, first + j, range(1, REACH - j))
        return carry

    lax.fori_loop(0, STEP, one_chunk, 0)


def inner_kernel(head, inner, tail, out_ref, rows_ref):
    sign, first_chunk = pl.program_id(0), pl.program_id(1) * STEP

    def one_chunk(c, carry):
        load_rows(rows_ref, 0, head.at[sign, first_chunk + c])
        load_rows(rows_ref, REACH, inner.at[sign, first_chunk + c])
        load_rows(rows_ref, 3 * REACH, tail.at[sign, first_chunk + c])
        for s in range(3 * REACH):
            out_ref[c, s] = cross_tile(rows_ref, s, range(max(1, REACH - s), REACH + 1))
        return carry

    lax.fori_loop(0, STEP, one_chunk, 0)


def final_kernel(before, head, tail, after, outer_ref, inner_ref, valid_ref, out_ref, rows_ref):
    shape = (REACH, LANES)
    lane = lax.broadcasted_iota(jnp.int32, shape, 1)
    row = lax.broadcasted_iota(jnp.int32, shape, 0)
    mirror = pl.program_id(0) == 1
    order = jnp.where(mirror, (LANES - lane) % LANES, lane)
    slots = out_ref.shape[0]

    first_chunk = pl.program_id(1) * STEP
    first_sums = pl.program_id(0) * CHUNKS + first_chunk

    def one_chunk(c, carry):
        at = jnp.where(mirror, STEP - 1 - c, c)
        lanes = pl.ds(pl.multiple_of(at * LANES, LANES), LANES)
        load_rows(rows_ref, 0, before.at[0, c])
        load_rows(rows_ref, REACH, head.at[pl.program_id(0), first_chunk + c])
        load_rows(rows_ref, 2 * REACH, tail.at[pl.program_id(0), first_chunk + c])
        load_rows(rows_ref, 3 * REACH, after.at[0, c])
        powers = {}
        for s in range(-REACH, slots):
            terms = []
            if s < 0 or s >= slots - REACH:
                j = s % REACH
                start = j if s < 0 else 2 * REACH + j
                terms.append(cross_tile(rows_ref, start, range(REACH - j, REACH + 1)))
            if s in OUTER:
                terms.append(outer_ref[first_sums + c, OUTER.index(s)])
            if 0 <= s < slots - REACH:
                terms.append(inner_ref[first_sums + c, s])
            value = jnp.take_along_axis(sum(terms[1:], terms[0]), order, axis=1)
            powers[s] = jnp.where(valid_ref[s + REACH] > 0.0, value * (1.0 / 64.0), 0.0)
            if s >= 0:
                out_ref[s, pl.ds(0, REACH), lanes] = powers[s]
                backward = powers[s - 1]
                for k in range(2, REACH + 1):
                    backward = jnp.where(row == k - 1, powers[s - k], backward)
                out_ref[s, pl.ds(REACH, REACH), lanes] = backward
        return carry

    lax.fori_loop(0, STEP, one_chunk, 0)


CHUNKS, STEP = 4, 2


def cross_call(kernel, name, operands, specs, out_specs, out_shape, held, pairs):
    rows = 128
    return pl.pallas_call(
        kernel,
        grid=(2, CHUNKS // STEP),
        in_specs=specs,
        out_specs=out_specs,
        out_shape=out_shape,
        scratch_shapes=[pltpu.VMEM((held, rows, LANES), jnp.float32)],
        compiler_params=pltpu.CompilerParams(vmem_limit_bytes=32 * MIB),
        cost_estimate=pl.CostEstimate(
            flops=2 * pairs * rows * 1024,
            bytes_accessed=2 * held * rows * 1024,
            transcendentals=0,
        ),
        name=name,
    )(*operands)


def chunks_spec(array):
    return pl.BlockSpec((1, STEP) + array.shape[2:], lambda i, j: (i, j, 0, 0, 0))


def whole():
    return pl.BlockSpec(memory_space=pltpu.VMEM)


def sums_spec(slots):
    return pl.BlockSpec(
        (STEP, slots, REACH, LANES), lambda i, j: (i * (CHUNKS // STEP) + j, 0, 0, 0)
    )


def outer_powers(head, tail):
    slots = 2 * REACH
    return cross_call(
        outer_kernel,
        "outer_pairs",
        [head, tail],
        [whole()] * 2,
        sums_spec(slots),
        jax.ShapeDtypeStruct((2 * CHUNKS, slots, REACH, LANES), jnp.float32),
        slots,
        56,
    )


def inner_powers(head, inner, tail):
    slots = 3 * REACH
    return cross_call(
        inner_kernel,
        "inner_pairs",
        [head, inner, tail],
        [whole()] * 3,
        sums_spec(slots),
        jax.ShapeDtypeStruct((2 * CHUNKS, slots, REACH, LANES), jnp.float32),
        4 * REACH,
        164,
    )


def final_powers(before, head, tail, after, outer_sums, inner_sums, valid):
    slots = 4 * REACH
    operands = [before, head, tail, after, outer_sums, inner_sums, valid]
    return cross_call(
        final_kernel,
        "pair_power",
        operands,
        [chunks_spec(before), whole(), whole(), chunks_spec(after), whole(), whole(), whole()],
        pl.BlockSpec(
            (slots, 2 * REACH, STEP * LANES),
            lambda i, j: (0, 0, jnp.where(i == 0, j, 2 * CHUNKS // STEP - 1 - j)),
        ),
        jax.ShapeDtypeStruct((slots, 2 * REACH, 2 * CHUNKS * LANES), jnp.float32),
        slots,
        72,
    )


def after_those(arrays, *earlier):
    def kernel(*refs):
        pass

    count = len(arrays)
    anywhere = pl.BlockSpec(memory_space=pl.ANY)
    return pl.pallas_call(
        kernel,
        in_specs=[anywhere] * (count + len(earlier)),
        out_specs=[anywhere] * count,
        out_shape=[jax.ShapeDtypeStruct(array.shape, array.dtype) for array in arrays],
        input_output_aliases={i: i for i in range(count)},
        name="in_order",
    )(*arrays, *earlier)


def body(visibilities, owner_order, group_ids, partner_flags):
    n_tm = lax.axis_size("tm")
    n_chan = lax.axis_size("chan")
    n_dev = n_tm * n_chan
    count, n_base, _, width = visibilities.shape
    per = n_base // n_dev

    table = half_table(width * n_chan)

    start = lax.axis_index(AXES) * per
    groups = lax.dynamic_slice_in_dim(
        jnp.pad(group_ids, (REACH, REACH), constant_values=-1), start, per + 2 * REACH, 0
    )
    flags = lax.dynamic_slice_in_dim(
        jnp.pad(partner_flags, ((REACH, REACH), (0, 0))), start, per + REACH, 0
    )
    own_group = groups[: per + REACH]
    same = jnp.stack([groups[k : k + per + REACH] == own_group for k in range(1, REACH + 1)], 1)
    valid = jnp.broadcast_to(
        (same & (flags == 1)).astype(jnp.float32)[:, :, None], (per + REACH, REACH, LANES)
    )

    def exchange(slots, earlier):
        send = gather(visibilities, owner_order, slots, n_dev, earlier)
        send = send.reshape(n_dev, 2 * count * len(slots), width)
        return lax.all_to_all(send, AXES, 0, 0, tiled=True)

    up = [(i, i + 1) for i in range(n_dev - 1)]
    down = [(i + 1, i) for i in range(n_dev - 1)]
    received_outer = exchange(OUTER, group_ids)
    received_inner = exchange(INNER, group_ids)
    head = spectra(received_outer, table, n_tm, n_chan, 0, REACH, group_ids)
    tail = spectra(received_outer, table, n_tm, n_chan, REACH, REACH, group_ids)
    outer_sums = outer_powers(head, tail)
    head_sent, tail_sent = after_those((head, tail), outer_sums, valid)
    after = lax.ppermute(head_sent, AXES, down)
    before = lax.ppermute(tail_sent, AXES, up)
    inner = spectra(received_inner, table, n_tm, n_chan, 0, 2 * REACH, outer_sums)
    inner_sums = inner_powers(head_sent, inner, tail_sent)
    return final_powers(before, head_sent, tail_sent, after, outer_sums, inner_sums, valid)


def solution(mesh):
    return jax.shard_map(
        body,
        mesh=mesh,
        in_specs=(P("tm", None, None, "chan"), P(), P(), P()),
        out_specs=P(AXES, None, None),
        check_vma=False,
    )
```

```python
import functools
import math

import jax
import jax.numpy as jnp
from jax import lax
from jax.experimental import pallas as pl
from jax.experimental.pallas import tpu as pltpu
from jax.sharding import PartitionSpec as P

AXES = ("tm", "chan")
MIB = 2**20
LANES = 128
REACH = 8
OUTER = tuple(range(8)) + tuple(range(24, 32))
INNER = tuple(range(8, 24))


def in_hbm(array):
    return pltpu.with_memory_space_constraint(array, pltpu.HBM)


def half_table(n_chan):
    channel_index = jnp.arange(n_chan, dtype=jnp.int32)
    place = jnp.arange(n_chan, dtype=jnp.int32)
    delay_index = place // (2 * LANES) * LANES + place % LANES
    is_sine = place % (2 * LANES) >= LANES
    middle = is_sine & (delay_index == 0)
    delay_index = jnp.where(middle, n_chan // 2, delay_index)
    turn = jnp.where(is_sine & ~middle, 3 * n_chan // 4, 0)
    phase_index = (channel_index[:, None] * delay_index[None, :] + turn[None, :]) % n_chan
    phase_angle = 2.0 * math.pi / n_chan * phase_index.astype(jnp.float32)
    base_angle = 2.0 * math.pi / n_chan * channel_index.astype(jnp.float32)
    window_taper = (
        0.35875
        - 0.48829 * jnp.cos(base_angle)
        + 0.14128 * jnp.cos(2.0 * base_angle)
        - 0.01168 * jnp.cos(3.0 * base_angle)
    )
    weights_norm = window_taper / jnp.sqrt(jnp.sum(window_taper * window_taper))
    return (weights_norm[:, None] * jnp.cos(phase_angle)).astype(jnp.bfloat16)


def gather_kernel(slots, per, order_ref, vis_ref, _, out_ref, vis, rows, load_sems, store_sems):
    count = vis.shape[0]
    half = count // 2
    loads = [
        pltpu.make_async_copy(
            vis_ref.at[pl.ds(h * half, half)], vis.at[pl.ds(h * half, half)], load_sems.at[h]
        )
        for h in range(2)
    ]
    for load in loads:
        load.start()
    n_dev = out_ref.shape[0]
    groups = store_sems.shape[0]
    owners = n_dev // groups

    def sort_half(h, first, number):
        def one_owner(i, carry):
            owner = first + i
            base = owner * per
            for j, slot in enumerate(slots):
                source = order_ref[base + slot]
                for t in range(h * half, (h + 1) * half):
                    rows[owner, j, t] = vis[t, source]
            return carry

        lax.fori_loop(0, number, one_owner, 0)

    loads[0].wait()
    sort_half(0, 0, n_dev)
    loads[1].wait()
    stores = []
    for g in range(groups):
        sort_half(1, g * owners, owners)
        span = pl.ds(g * owners, owners)
        store = pltpu.make_async_copy(rows.at[span], out_ref.at[span], store_sems.at[g])
        store.start()
        stores.append(store)
    for store in stores:
        store.wait()


def gather(visibilities, order, slots, n_dev, earlier):
    count, n_base = visibilities.shape[:2]
    tail = visibilities.shape[2:]
    groups = 8
    shape = (n_dev, len(slots), count) + tail
    anywhere = pl.BlockSpec(memory_space=pl.ANY)
    return pl.pallas_call(
        functools.partial(gather_kernel, slots, n_base // n_dev),
        grid_spec=pltpu.PrefetchScalarGridSpec(
            num_scalar_prefetch=1,
            grid=(),
            in_specs=[anywhere] * 2,
            out_specs=anywhere,
            scratch_shapes=[
                pltpu.VMEM(visibilities.shape, visibilities.dtype),
                pltpu.VMEM(shape, visibilities.dtype),
                pltpu.SemaphoreType.DMA((2,)),
                pltpu.SemaphoreType.DMA((groups,)),
            ],
        ),
        out_shape=pltpu.HBM(shape, visibilities.dtype),
        compiler_params=pltpu.CompilerParams(vmem_limit_bytes=24 * MIB),
        cost_estimate=pl.CostEstimate(
            flops=0, bytes_accessed=2 * count * n_dev * len(slots) * 512, transcendentals=0
        ),
        name="slot_gather",
    )(in_hbm(order), in_hbm(visibilities), in_hbm(earlier))


def spectra_kernel(received_ref, table_ref, _, out_ref):
    sources, n_chan, rows = received_ref.shape[:3]
    slots = out_ref.shape[2]
    n_rows = sources * rows
    block = jnp.concatenate(
        [received_ref[:, c].reshape(n_rows, LANES) for c in range(n_chan)], axis=1
    )
    chunks = table_ref.shape[1] // (2 * LANES)
    shape = (n_rows // 8, 8, LANES)
    first = lax.broadcasted_iota(jnp.int32, shape, 2) == 0
    is_real = lax.broadcasted_iota(jnp.int32, shape, 1) % 2 == 0

    def store(sign, c, value):
        value = jnp.swapaxes(value.reshape(sources, slots, 8, LANES), 0, 1)
        value = value.reshape(slots, sources * 8, LANES).astype(jnp.bfloat16)
        out_ref[sign, c] = value

    minus = []
    for c in range(chunks):
        both = jnp.dot(
            block, table_ref[:, pl.ds(2 * c * LANES, 2 * LANES)], preferred_element_type=jnp.float32
        )
        cosine, sine = both[:, :LANES].reshape(shape), both[:, LANES:].reshape(shape)
        other = jnp.where(is_real, pltpu.roll(sine, 7, 1), -pltpu.roll(sine, 1, 1))
        ahead, back = cosine + other, cosine - other
        if c == 0:
            ahead, back = jnp.where(first, cosine, ahead), jnp.where(first, sine, back)
        store(0, c, ahead)
        minus.append(back)
        if c > 0:
            store(1, c - 1, jnp.where(first, back, minus[c - 1]))
    store(1, chunks - 1, jnp.where(first, minus[0], minus[-1]))


def spectra(received, table, n_tm, n_chan, first, slots, earlier, stays):
    _, pairs, lanes = received.shape
    step = REACH
    width = table.shape[1]
    rows = n_tm * 8
    chunks = width // (2 * LANES)
    return pl.pallas_call(
        spectra_kernel,
        grid=(slots // step,),
        in_specs=[
            pl.BlockSpec(
                (n_tm, n_chan, 8 * step, lanes), lambda t: (0, 0, first // step + t, 0)
            ),
            whole()
            if stays
            else pl.BlockSpec(table.shape, lambda t: (0, 0), pipeline_mode=pl.Buffered(1)),
            pl.BlockSpec(memory_space=pl.ANY),
        ],
        out_specs=pl.BlockSpec((2, chunks, step, rows, LANES), lambda t: (0, 0, t, 0, 0)),
        out_shape=(jax.ShapeDtypeStruct if stays else pltpu.HBM)(
            (2, chunks, slots, rows, LANES), jnp.bfloat16
        ),
        compiler_params=pltpu.CompilerParams(vmem_limit_bytes=32 * MIB),
        cost_estimate=pl.CostEstimate(
            flops=16 * slots * n_tm * width * width,
            bytes_accessed=64 * slots * n_tm * width,
            transcendentals=0,
        ),
        name="delay_spectra",
    )(
        in_hbm(received.reshape(n_tm, n_chan, pairs, lanes)),
        table if stays else in_hbm(table),
        earlier,
    )


def fold_rows(sums):
    row = lax.broadcasted_iota(jnp.int32, sums[0].shape, 0)
    for bit in (1, 2, 4):
        low = (row & bit) == 0
        merged = []
        for i in range(0, len(sums), 2):
            a, b = sums[i], sums[i + 1]
            kept, moved = jnp.where(low, a, b), jnp.where(low, b, a)
            merged.append(kept + pltpu.roll(moved, 8 - bit, 0))
        sums = merged
    return sums[0]


def cross_tile(rows_ref, s, offsets):
    spans = [pl.ds(8 * g, 8) for g in range(rows_ref.shape[1] // 8)]
    own = [rows_ref[s, span] for span in spans]
    sums = []
    for k in range(1, REACH + 1):
        if k not in offsets:
            sums.append(jnp.zeros((8, LANES), jnp.float32))
            continue
        total = None
        for g, span in enumerate(spans):
            term = own[g] * rows_ref[s + k, span]
            total = term if total is None else total + term
        sums.append(total)
    return fold_rows(sums)


def load_rows(target, at, source):
    target[pl.ds(at, source.shape[0])] = source[...].astype(jnp.float32)


def outer_kernel(head, tail, out_ref, rows_ref):
    def one_chunk(c, carry):
        load_rows(rows_ref, 0, head.at[0, c])
        load_rows(rows_ref, REACH, tail.at[0, c])
        for first in (0, REACH):
            for j in range(REACH):
                out_ref[c, first + j] = cross_tile(rows_ref, first + j, range(1, REACH - j))
        return carry

    lax.fori_loop(0, STEP, one_chunk, 0)


def inner_kernel(head, inner, tail, out_ref, rows_ref):
    sign, first_chunk = pl.program_id(0), pl.program_id(1) * STEP

    def one_chunk(c, carry):
        load_rows(rows_ref, 0, head.at[sign, first_chunk + c])
        load_rows(rows_ref, REACH, inner.at[sign, first_chunk + c])
        load_rows(rows_ref, 3 * REACH, tail.at[sign, first_chunk + c])
        for s in range(3 * REACH):
            out_ref[c, s] = cross_tile(rows_ref, s, range(max(1, REACH - s), REACH + 1))
        return carry

    lax.fori_loop(0, STEP, one_chunk, 0)


def final_kernel(before, head, tail, after, outer_ref, inner_ref, valid_ref, out_ref, rows_ref):
    shape = (REACH, LANES)
    lane = lax.broadcasted_iota(jnp.int32, shape, 1)
    row = lax.broadcasted_iota(jnp.int32, shape, 0)
    mirror = pl.program_id(0) == 1
    order = jnp.where(mirror, (LANES - lane) % LANES, lane)
    slots = out_ref.shape[0]

    first_chunk = pl.program_id(1) * STEP
    first_sums = pl.program_id(0) * CHUNKS + first_chunk

    def one_chunk(c, carry):
        at = jnp.where(mirror, STEP - 1 - c, c)
        lanes = pl.ds(pl.multiple_of(at * LANES, LANES), LANES)
        load_rows(rows_ref, 0, before.at[0, c])
        load_rows(rows_ref, REACH, head.at[pl.program_id(0), first_chunk + c])
        load_rows(rows_ref, 2 * REACH, tail.at[pl.program_id(0), first_chunk + c])
        load_rows(rows_ref, 3 * REACH, after.at[0, c])
        powers = {}
        for s in range(-REACH, slots):
            terms = []
            if s < 0 or s >= slots - REACH:
                j = s % REACH
                start = j if s < 0 else 2 * REACH + j
                terms.append(cross_tile(rows_ref, start, range(REACH - j, REACH + 1)))
            if s in OUTER:
                terms.append(outer_ref[first_sums + c, OUTER.index(s)])
            if 0 <= s < slots - REACH:
                terms.append(inner_ref[first_sums + c, s])
            value = jnp.take_along_axis(sum(terms[1:], terms[0]), order, axis=1)
            powers[s] = jnp.where(valid_ref[s + REACH] > 0.0, value * (1.0 / 64.0), 0.0)
            if s >= 0:
                out_ref[s, pl.ds(0, REACH), lanes] = powers[s]
                backward = powers[s - 1]
                for k in range(2, REACH + 1):
                    backward = jnp.where(row == k - 1, powers[s - k], backward)
                out_ref[s, pl.ds(REACH, REACH), lanes] = backward
        return carry

    lax.fori_loop(0, STEP, one_chunk, 0)


CHUNKS, STEP = 4, 2


def cross_call(kernel, name, operands, specs, out_specs, out_shape, held, pairs):
    rows = 128
    return pl.pallas_call(
        kernel,
        grid=(2, CHUNKS // STEP),
        in_specs=specs,
        out_specs=out_specs,
        out_shape=out_shape,
        scratch_shapes=[pltpu.VMEM((held, rows, LANES), jnp.float32)],
        compiler_params=pltpu.CompilerParams(vmem_limit_bytes=32 * MIB),
        cost_estimate=pl.CostEstimate(
            flops=2 * pairs * rows * 1024,
            bytes_accessed=2 * held * rows * 1024,
            transcendentals=0,
        ),
        name=name,
    )(*operands)


def chunks_spec(array):
    return pl.BlockSpec((1, STEP) + array.shape[2:], lambda i, j: (i, j, 0, 0, 0))


def whole():
    return pl.BlockSpec(memory_space=pltpu.VMEM)


def sums_spec(slots):
    return pl.BlockSpec(
        (STEP, slots, REACH, LANES), lambda i, j: (i * (CHUNKS // STEP) + j, 0, 0, 0)
    )


def outer_powers(head, tail):
    slots = 2 * REACH
    return cross_call(
        outer_kernel,
        "outer_pairs",
        [in_hbm(head), in_hbm(tail)],
        [chunks_spec(head)] * 2,
        sums_spec(slots),
        jax.ShapeDtypeStruct((2 * CHUNKS, slots, REACH, LANES), jnp.float32),
        slots,
        56,
    )


def inner_powers(head, inner, tail):
    slots = 3 * REACH
    return cross_call(
        inner_kernel,
        "inner_pairs",
        [head, inner, tail],
        [whole()] * 3,
        sums_spec(slots),
        jax.ShapeDtypeStruct((2 * CHUNKS, slots, REACH, LANES), jnp.float32),
        4 * REACH,
        164,
    )


def final_powers(before, head, tail, after, outer_sums, inner_sums, valid):
    slots = 4 * REACH
    operands = [before, head, tail, after, outer_sums, inner_sums, valid]
    return cross_call(
        final_kernel,
        "pair_power",
        operands,
        [chunks_spec(before), whole(), whole(), chunks_spec(after), whole(), whole(), whole()],
        pl.BlockSpec(
            (slots, 2 * REACH, STEP * LANES),
            lambda i, j: (0, 0, jnp.where(i == 0, j, 2 * CHUNKS // STEP - 1 - j)),
        ),
        jax.ShapeDtypeStruct((slots, 2 * REACH, 2 * CHUNKS * LANES), jnp.float32),
        slots,
        72,
    )


def after_those(arrays, *earlier):
    def kernel(*refs):
        pass

    count = len(arrays)
    anywhere = pl.BlockSpec(memory_space=pl.ANY)
    return pl.pallas_call(
        kernel,
        in_specs=[anywhere] * (count + len(earlier)),
        out_specs=[anywhere] * count,
        out_shape=[pltpu.HBM(array.shape, array.dtype) for array in arrays],
        input_output_aliases={i: i for i in range(count)},
        name="in_order",
    )(*[in_hbm(array) for array in arrays], *earlier)


def body(visibilities, owner_order, group_ids, partner_flags):
    n_tm = lax.axis_size("tm")
    n_chan = lax.axis_size("chan")
    n_dev = n_tm * n_chan
    count, n_base, _, width = visibilities.shape
    per = n_base // n_dev

    table = half_table(width * n_chan)

    start = lax.axis_index(AXES) * per
    groups = lax.dynamic_slice_in_dim(
        jnp.pad(group_ids, (REACH, REACH), constant_values=-1), start, per + 2 * REACH, 0
    )
    flags = lax.dynamic_slice_in_dim(
        jnp.pad(partner_flags, ((REACH, REACH), (0, 0))), start, per + REACH, 0
    )
    own_group = groups[: per + REACH]
    same = jnp.stack([groups[k : k + per + REACH] == own_group for k in range(1, REACH + 1)], 1)
    valid = jnp.broadcast_to(
        (same & (flags == 1)).astype(jnp.float32)[:, :, None], (per + REACH, REACH, LANES)
    )

    def exchange(slots, earlier):
        send = gather(visibilities, owner_order, slots, n_dev, earlier)
        send = send.reshape(n_dev, 2 * count * len(slots), width)
        return lax.all_to_all(send, AXES, 0, 0, tiled=True)

    up = [(i, i + 1) for i in range(n_dev - 1)]
    down = [(i + 1, i) for i in range(n_dev - 1)]
    received_outer = exchange(OUTER, group_ids)
    received_inner = exchange(INNER, group_ids)
    head = spectra(received_outer, table, n_tm, n_chan, 0, REACH, group_ids, False)
    tail = spectra(received_outer, table, n_tm, n_chan, REACH, REACH, group_ids, False)
    outer_sums = outer_powers(head, tail)
    head_sent, tail_sent = after_those((head, tail), outer_sums, valid)
    after = lax.ppermute(head_sent, AXES, down)
    before = lax.ppermute(tail_sent, AXES, up)
    inner = spectra(received_inner, table, n_tm, n_chan, 0, 2 * REACH, outer_sums, True)
    inner_sums = inner_powers(head_sent, inner, tail_sent)
    return final_powers(before, head_sent, tail_sent, after, outer_sums, inner_sums, valid)


def solution(mesh):
    return jax.shard_map(
        body,
        mesh=mesh,
        in_specs=(P("tm", None, None, "chan"), P(), P(), P()),
        out_specs=P(AXES, None, None),
        check_vma=False,
    )
```

```python
import functools
import math

import jax
import jax.numpy as jnp
from jax import lax
from jax.experimental import pallas as pl
from jax.experimental.pallas import tpu as pltpu
from jax.sharding import PartitionSpec as P

AXES = ("tm", "chan")
MIB = 2**20
LANES = 128
REACH = 8
OUTER = tuple(range(8)) + tuple(range(24, 32))
INNER = tuple(range(8, 24))


def in_hbm(array):
    return pltpu.with_memory_space_constraint(array, pltpu.HBM)


def half_table(n_chan):
    channel_index = jnp.arange(n_chan, dtype=jnp.int32)
    place = jnp.arange(n_chan, dtype=jnp.int32)
    delay_index = place // (2 * LANES) * LANES + place % LANES
    is_sine = place % (2 * LANES) >= LANES
    middle = is_sine & (delay_index == 0)
    delay_index = jnp.where(middle, n_chan // 2, delay_index)
    turn = jnp.where(is_sine & ~middle, 3 * n_chan // 4, 0)
    phase_index = (channel_index[:, None] * delay_index[None, :] + turn[None, :]) % n_chan
    phase_angle = 2.0 * math.pi / n_chan * phase_index.astype(jnp.float32)
    base_angle = 2.0 * math.pi / n_chan * channel_index.astype(jnp.float32)
    window_taper = (
        0.35875
        - 0.48829 * jnp.cos(base_angle)
        + 0.14128 * jnp.cos(2.0 * base_angle)
        - 0.01168 * jnp.cos(3.0 * base_angle)
    )
    weights_norm = window_taper / jnp.sqrt(jnp.sum(window_taper * window_taper))
    return (weights_norm[:, None] * jnp.cos(phase_angle)).astype(jnp.bfloat16)


def gather_kernel(slots, per, order_ref, vis_ref, _, out_ref, vis, rows, load_sems, store_sems):
    count = vis.shape[0]
    half = count // 2
    loads = [
        pltpu.make_async_copy(
            vis_ref.at[pl.ds(h * half, half)], vis.at[pl.ds(h * half, half)], load_sems.at[h]
        )
        for h in range(2)
    ]
    for load in loads:
        load.start()
    n_dev = out_ref.shape[0]
    groups = store_sems.shape[0]
    owners = n_dev // groups

    def sort_half(h, first, number):
        def one_owner(i, carry):
            owner = first + i
            base = owner * per
            for j, slot in enumerate(slots):
                source = order_ref[base + slot]
                for t in range(h * half, (h + 1) * half):
                    rows[owner, j, t] = vis[t, source]
            return carry

        lax.fori_loop(0, number, one_owner, 0)

    loads[0].wait()
    sort_half(0, 0, n_dev)
    loads[1].wait()
    stores = []
    for g in range(groups):
        sort_half(1, g * owners, owners)
        span = pl.ds(g * owners, owners)
        store = pltpu.make_async_copy(rows.at[span], out_ref.at[span], store_sems.at[g])
        store.start()
        stores.append(store)
    for store in stores:
        store.wait()


def gather(visibilities, order, slots, n_dev, earlier):
    count, n_base = visibilities.shape[:2]
    tail = visibilities.shape[2:]
    groups = 8
    shape = (n_dev, len(slots), count) + tail
    anywhere = pl.BlockSpec(memory_space=pl.ANY)
    return pl.pallas_call(
        functools.partial(gather_kernel, slots, n_base // n_dev),
        grid_spec=pltpu.PrefetchScalarGridSpec(
            num_scalar_prefetch=1,
            grid=(),
            in_specs=[anywhere] * 2,
            out_specs=anywhere,
            scratch_shapes=[
                pltpu.VMEM(visibilities.shape, visibilities.dtype),
                pltpu.VMEM(shape, visibilities.dtype),
                pltpu.SemaphoreType.DMA((2,)),
                pltpu.SemaphoreType.DMA((groups,)),
            ],
        ),
        out_shape=pltpu.HBM(shape, visibilities.dtype),
        compiler_params=pltpu.CompilerParams(vmem_limit_bytes=24 * MIB),
        cost_estimate=pl.CostEstimate(
            flops=0, bytes_accessed=2 * count * n_dev * len(slots) * 512, transcendentals=0
        ),
        name="slot_gather",
    )(in_hbm(order), in_hbm(visibilities), in_hbm(earlier))


def spectra_kernel(received_ref, table_ref, _, out_ref):
    sources, n_chan, rows = received_ref.shape[:3]
    slots = out_ref.shape[2]
    n_rows = sources * rows
    block = jnp.concatenate(
        [received_ref[:, c].reshape(n_rows, LANES) for c in range(n_chan)], axis=1
    )
    chunks = table_ref.shape[1] // (2 * LANES)
    shape = (n_rows // 8, 8, LANES)
    first = lax.broadcasted_iota(jnp.int32, shape, 2) == 0
    is_real = lax.broadcasted_iota(jnp.int32, shape, 1) % 2 == 0

    def store(sign, c, value):
        value = jnp.swapaxes(value.reshape(sources, slots, 8, LANES), 0, 1)
        value = value.reshape(slots, sources * 8, LANES).astype(jnp.bfloat16)
        out_ref[sign, c] = value

    minus = []
    for c in range(chunks):
        both = jnp.dot(
            block, table_ref[:, pl.ds(2 * c * LANES, 2 * LANES)], preferred_element_type=jnp.float32
        )
        cosine, sine = both[:, :LANES].reshape(shape), both[:, LANES:].reshape(shape)
        other = jnp.where(is_real, pltpu.roll(sine, 7, 1), -pltpu.roll(sine, 1, 1))
        ahead, back = cosine + other, cosine - other
        if c == 0:
            ahead, back = jnp.where(first, cosine, ahead), jnp.where(first, sine, back)
        store(0, c, ahead)
        minus.append(back)
        if c > 0:
            store(1, c - 1, jnp.where(first, back, minus[c - 1]))
    store(1, chunks - 1, jnp.where(first, minus[0], minus[-1]))


def spectra(received, table, n_tm, n_chan, first, slots, earlier, stays):
    _, pairs, lanes = received.shape
    step = REACH
    width = table.shape[1]
    rows = n_tm * 8
    chunks = width // (2 * LANES)
    return pl.pallas_call(
        spectra_kernel,
        grid=(slots // step,),
        in_specs=[
            pl.BlockSpec(
                (n_tm, n_chan, 8 * step, lanes), lambda t: (0, 0, first // step + t, 0)
            ),
            whole()
            if stays
            else pl.BlockSpec(table.shape, lambda t: (0, 0), pipeline_mode=pl.Buffered(1)),
            pl.BlockSpec(memory_space=pl.ANY),
        ],
        out_specs=pl.BlockSpec((2, chunks, step, rows, LANES), lambda t: (0, 0, t, 0, 0)),
        out_shape=(jax.ShapeDtypeStruct if stays else pltpu.HBM)(
            (2, chunks, slots, rows, LANES), jnp.bfloat16
        ),
        compiler_params=pltpu.CompilerParams(vmem_limit_bytes=32 * MIB),
        cost_estimate=pl.CostEstimate(
            flops=16 * slots * n_tm * width * width,
            bytes_accessed=64 * slots * n_tm * width,
            transcendentals=0,
        ),
        name="delay_spectra",
    )(
        in_hbm(received.reshape(n_tm, n_chan, pairs, lanes)),
        table if stays else in_hbm(table),
        earlier,
    )


def fold_rows(sums):
    row = lax.broadcasted_iota(jnp.int32, sums[0].shape, 0)
    for bit in (1, 2, 4):
        low = (row & bit) == 0
        merged = []
        for i in range(0, len(sums), 2):
            a, b = sums[i], sums[i + 1]
            kept, moved = jnp.where(low, a, b), jnp.where(low, b, a)
            merged.append(kept + pltpu.roll(moved, 8 - bit, 0))
        sums = merged
    return sums[0]


def cross_tile(rows_ref, s, offsets):
    spans = [pl.ds(8 * g, 8) for g in range(rows_ref.shape[1] // 8)]
    own = [rows_ref[s, span] for span in spans]
    sums = []
    for k in range(1, REACH + 1):
        if k not in offsets:
            sums.append(jnp.zeros((8, LANES), jnp.float32))
            continue
        total = None
        for g, span in enumerate(spans):
            term = own[g] * rows_ref[s + k, span]
            total = term if total is None else total + term
        sums.append(total)
    return fold_rows(sums)


def load_rows(target, at, source):
    target[pl.ds(at, source.shape[0])] = source[...].astype(jnp.float32)


def outer_kernel(head, tail, out_ref, rows_ref):
    def one_chunk(c, carry):
        load_rows(rows_ref, 0, head.at[0, c])
        load_rows(rows_ref, REACH, tail.at[0, c])
        for first in (0, REACH):
            for j in range(REACH):
                out_ref[c, first + j] = cross_tile(rows_ref, first + j, range(1, REACH - j))
        return carry

    lax.fori_loop(0, STEP, one_chunk, 0)


def inner_kernel(head, inner, tail, out_ref, rows_ref):
    sign, first_chunk = pl.program_id(0), pl.program_id(1) * STEP

    def one_chunk(c, carry):
        load_rows(rows_ref, 0, head.at[sign, first_chunk + c])
        load_rows(rows_ref, REACH, inner.at[sign, first_chunk + c])
        load_rows(rows_ref, 3 * REACH, tail.at[sign, first_chunk + c])
        for s in range(3 * REACH):
            out_ref[c, s] = cross_tile(rows_ref, s, range(max(1, REACH - s), REACH + 1))
        return carry

    lax.fori_loop(0, STEP, one_chunk, 0)


def final_kernel(
    before, head, tail, after, outer_ref, inner_ref, valid_ref, out_ref, rows_ref, near, sems
):
    shape = (REACH, LANES)
    lane = lax.broadcasted_iota(jnp.int32, shape, 1)
    row = lax.broadcasted_iota(jnp.int32, shape, 0)
    mirror = pl.program_id(0) == 1
    order = jnp.where(mirror, (LANES - lane) % LANES, lane)
    slots = out_ref.shape[0]

    steps = CHUNKS // STEP
    step = pl.program_id(0) * steps + pl.program_id(1)

    def arrival(side, number):
        source = (before, after)[side]
        span = pl.ds(number % steps * STEP, STEP)
        return pltpu.make_async_copy(
            source.at[number // steps, span], near.at[side, number], sems.at[side, number]
        )

    @pl.when(step == 0)
    def _():
        for number in range(2 * steps):
            for side in range(2):
                arrival(side, number).start()

    for side in range(2):
        arrival(side, step).wait()
    first_chunk = pl.program_id(1) * STEP
    first_sums = pl.program_id(0) * CHUNKS + first_chunk

    def one_chunk(c, carry):
        at = jnp.where(mirror, STEP - 1 - c, c)
        lanes = pl.ds(pl.multiple_of(at * LANES, LANES), LANES)
        load_rows(rows_ref, 0, near.at[0, step, c])
        load_rows(rows_ref, REACH, head.at[pl.program_id(0), first_chunk + c])
        load_rows(rows_ref, 2 * REACH, tail.at[pl.program_id(0), first_chunk + c])
        load_rows(rows_ref, 3 * REACH, near.at[1, step, c])
        powers = {}
        for s in range(-REACH, slots):
            terms = []
            if s < 0 or s >= slots - REACH:
                j = s % REACH
                start = j if s < 0 else 2 * REACH + j
                terms.append(cross_tile(rows_ref, start, range(REACH - j, REACH + 1)))
            if s in OUTER:
                terms.append(outer_ref[first_sums + c, OUTER.index(s)])
            if 0 <= s < slots - REACH:
                terms.append(inner_ref[first_sums + c, s])
            value = jnp.take_along_axis(sum(terms[1:], terms[0]), order, axis=1)
            powers[s] = jnp.where(valid_ref[s + REACH] > 0.0, value * (1.0 / 64.0), 0.0)
            if s >= 0:
                out_ref[s, pl.ds(0, REACH), lanes] = powers[s]
                backward = powers[s - 1]
                for k in range(2, REACH + 1):
                    backward = jnp.where(row == k - 1, powers[s - k], backward)
                out_ref[s, pl.ds(REACH, REACH), lanes] = backward
        return carry

    lax.fori_loop(0, STEP, one_chunk, 0)


CHUNKS, STEP = 4, 2


def cross_call(kernel, name, operands, specs, out_specs, out_shape, held, pairs, extra=()):
    rows = 128
    return pl.pallas_call(
        kernel,
        grid=(2, CHUNKS // STEP),
        in_specs=specs,
        out_specs=out_specs,
        out_shape=out_shape,
        scratch_shapes=[pltpu.VMEM((held, rows, LANES), jnp.float32), *extra],
        compiler_params=pltpu.CompilerParams(vmem_limit_bytes=32 * MIB),
        cost_estimate=pl.CostEstimate(
            flops=2 * pairs * rows * 1024,
            bytes_accessed=2 * held * rows * 1024,
            transcendentals=0,
        ),
        name=name,
    )(*operands)


def chunks_spec(array):
    return pl.BlockSpec((1, STEP) + array.shape[2:], lambda i, j: (i, j, 0, 0, 0))


def whole():
    return pl.BlockSpec(memory_space=pltpu.VMEM)


def sums_spec(slots):
    return pl.BlockSpec(
        (STEP, slots, REACH, LANES), lambda i, j: (i * (CHUNKS // STEP) + j, 0, 0, 0)
    )


def outer_powers(head, tail):
    slots = 2 * REACH
    return cross_call(
        outer_kernel,
        "outer_pairs",
        [in_hbm(head), in_hbm(tail)],
        [chunks_spec(head)] * 2,
        sums_spec(slots),
        jax.ShapeDtypeStruct((2 * CHUNKS, slots, REACH, LANES), jnp.float32),
        slots,
        56,
    )


def inner_powers(head, inner, tail):
    slots = 3 * REACH
    return cross_call(
        inner_kernel,
        "inner_pairs",
        [head, inner, tail],
        [whole()] * 3,
        sums_spec(slots),
        jax.ShapeDtypeStruct((2 * CHUNKS, slots, REACH, LANES), jnp.float32),
        4 * REACH,
        164,
    )


def final_powers(before, head, tail, after, outer_sums, inner_sums, valid):
    slots = 4 * REACH
    operands = [in_hbm(before), head, tail, in_hbm(after), outer_sums, inner_sums, valid]
    anywhere = pl.BlockSpec(memory_space=pl.ANY)
    near = (2, 2 * CHUNKS // STEP, STEP) + before.shape[2:]
    return cross_call(
        final_kernel,
        "pair_power",
        operands,
        [anywhere, whole(), whole(), anywhere, whole(), whole(), whole()],
        pl.BlockSpec(
            (slots, 2 * REACH, STEP * LANES),
            lambda i, j: (0, 0, jnp.where(i == 0, j, 2 * CHUNKS // STEP - 1 - j)),
        ),
        jax.ShapeDtypeStruct((slots, 2 * REACH, 2 * CHUNKS * LANES), jnp.float32),
        slots,
        72,
        [pltpu.VMEM(near, before.dtype), pltpu.SemaphoreType.DMA(near[:2])],
    )


def after_those(arrays, *earlier):
    def kernel(*refs):
        pass

    count = len(arrays)
    anywhere = pl.BlockSpec(memory_space=pl.ANY)
    return pl.pallas_call(
        kernel,
        in_specs=[anywhere] * (count + len(earlier)),
        out_specs=[anywhere] * count,
        out_shape=[pltpu.HBM(array.shape, array.dtype) for array in arrays],
        input_output_aliases={i: i for i in range(count)},
        name="in_order",
    )(*[in_hbm(array) for array in arrays], *earlier)


def body(visibilities, owner_order, group_ids, partner_flags):
    n_tm = lax.axis_size("tm")
    n_chan = lax.axis_size("chan")
    n_dev = n_tm * n_chan
    count, n_base, _, width = visibilities.shape
    per = n_base // n_dev

    table = half_table(width * n_chan)

    start = lax.axis_index(AXES) * per
    groups = lax.dynamic_slice_in_dim(
        jnp.pad(group_ids, (REACH, REACH), constant_values=-1), start, per + 2 * REACH, 0
    )
    flags = lax.dynamic_slice_in_dim(
        jnp.pad(partner_flags, ((REACH, REACH), (0, 0))), start, per + REACH, 0
    )
    own_group = groups[: per + REACH]
    same = jnp.stack([groups[k : k + per + REACH] == own_group for k in range(1, REACH + 1)], 1)
    valid = jnp.broadcast_to(
        (same & (flags == 1)).astype(jnp.float32)[:, :, None], (per + REACH, REACH, LANES)
    )

    def exchange(slots, earlier):
        send = gather(visibilities, owner_order, slots, n_dev, earlier)
        send = send.reshape(n_dev, 2 * count * len(slots), width)
        return lax.all_to_all(send, AXES, 0, 0, tiled=True)

    up = [(i, i + 1) for i in range(n_dev - 1)]
    down = [(i + 1, i) for i in range(n_dev - 1)]
    received_outer = exchange(OUTER, group_ids)
    received_inner = exchange(INNER, group_ids)
    head = spectra(received_outer, table, n_tm, n_chan, 0, REACH, group_ids, False)
    tail = spectra(received_outer, table, n_tm, n_chan, REACH, REACH, group_ids, False)
    outer_sums = outer_powers(head, tail)
    head_sent, tail_sent = after_those((head, tail), outer_sums, valid)
    after = lax.ppermute(head_sent, AXES, down)
    before = lax.ppermute(tail_sent, AXES, up)
    inner = spectra(received_inner, table, n_tm, n_chan, 0, 2 * REACH, outer_sums, True)
    inner_sums = inner_powers(head_sent, inner, tail_sent)
    return final_powers(before, head_sent, tail_sent, after, outer_sums, inner_sums, valid)


def solution(mesh):
    return jax.shard_map(
        body,
        mesh=mesh,
        in_specs=(P("tm", None, None, "chan"), P(), P(), P()),
        out_specs=P(AXES, None, None),
        check_vma=False,
    )
```
